256 devices in a mesh: blk: 16 (over y, x_hi, core), seq: 16 (over z, x_lo).
Axes of the slice: x: 4 (x_hi: 2, x_lo: 2; x = x_hi * 2 + x_lo), y: 4, z: 8, core: 2. Of those that a mesh axis runs over, the one named last changes fastest.
Arguments:
- saved_input: bfloat16 [16, 2048, 8192], P('blk', 'seq'), may hold values from -180 to 180
- output_grad: bfloat16 [16, 2048, 8192], P('blk', 'seq'), may hold values from -0.3984375 to 0.3984375
- weight_span: bfloat16 [16, 8192, 3, 256], P('blk', 'seq'), may hold values from -0.0625 to 0.0625
- grad_carry: float32 [16, 8192, 3, 256], P('blk', 'seq'), may hold values from -6 to 6
- attn_queries: bfloat16 [16, 2048, 4096], P('blk', 'seq'), may hold values from -6 to 6
- attn_keys: bfloat16 [16, 2048, 512], P('blk', 'seq'), may hold values from -6 to 6
- attn_values: bfloat16 [16, 2048, 512], P('blk', 'seq'), may hold values from -6 to 6
Outputs:
- carry_out: float32 [16, 8192, 3, 256], P('blk', 'seq')
- attn_out: bfloat16 [16, 2048, 4096], P('blk', 'seq')
The draws below stay inside these ranges and needn't reach their ends.
All inputs are finite; a program needn't handle non-finite values.
Results may differ from the reference program's by a relative error of at most 0.02.
Values may be sent and summed in bfloat16 or wider, within the bound.
No kernel may reach another device: no remote copies, remote signals or barrier semaphores. Data moves between devices by JAX's collectives and lax.ppermute only.
A program may use at most 192 MiB of HBM per device.

```python
import math
import jax
import jax.numpy as jnp
from jax import lax

D = 8192
HD = 128
FFC = 256
QH = 32
KVH = 4
WORKERS = 16
SEQ = 2048


def draw_saved_input(key, part):
    key = jax.random.fold_in(key, 3)
    subkeys = jax.random.split(key, 3)
    column_scale = jnp.exp(jax.random.uniform(subkeys[0], (1, 1, D), minval=math.log(0.3), maxval=math.log(3.0)))
    row_scale = jnp.exp(jax.random.uniform(subkeys[1], (WORKERS, SEQ, 1), minval=0.0, maxval=math.log(10.0)))
    entries = jax.random.truncated_normal(subkeys[2], -6.0, 6.0, (WORKERS, SEQ, D), jnp.float32)
    return (entries * column_scale * row_scale).astype(jnp.bfloat16)


def draw_attn_queries(key, part):
    key = jax.random.fold_in(key, 5)
    entries = jax.random.truncated_normal(key, -6.0, 6.0, (WORKERS, SEQ, QH * HD), jnp.float32)
    return entries.astype(jnp.bfloat16)


def draw_attn_keys(key, part):
    key = jax.random.fold_in(key, 7)
    entries = jax.random.truncated_normal(key, -6.0, 6.0, (WORKERS, SEQ, KVH, HD), jnp.float32)
    return entries.reshape(WORKERS, SEQ, KVH * HD).astype(jnp.bfloat16)


def spiked(array, key, source, target, shards_of, factor):
    owner, partner = [(jnp.arange(array.shape[position]) // (array.shape[position] // shards_of)).reshape([-1 if axis == position else 1 for axis in range(array.ndim)]) for position in (source, target)]
    chosen = jax.random.permutation(key, shards_of)[partner]
    strong = (owner == chosen) | (owner == (partner + shards_of // 2) % shards_of)
    return jnp.where(strong, factor * array, array)


def block_scale(rng, dims, cuts, least, largest):
    def one(position, parts):
        steps = jax.random.uniform(jax.random.fold_in(jax.random.fold_in(rng, 6), position), (parts,), jnp.float32, least / len(cuts), largest / len(cuts))
        return jnp.repeat(jnp.exp(steps), dims[position] // parts).reshape((-1,) + (1,) * (len(dims) - position - 1))

    loudness = one(*cuts[0])
    for cut in cuts[1:]:
        loudness = loudness * one(*cut)
    return loudness


def gaussian(key, extent, deviation, most, cuts=(), kind=jnp.bfloat16):
    gain = block_scale(key, extent, cuts, -0.22, 0.18) if cuts else 1.0
    array = jax.random.normal(key, extent, jnp.float32) * deviation * gain
    return jnp.minimum(jnp.maximum(array, -most), most).astype(kind)


def bell_draw_with(own_key, shape, scale, bound, cuts, heavy, kind=jnp.bfloat16):
    values = scale * jax.random.normal(own_key, shape, jnp.float32)
    if cuts:
        values = values * block_scale(own_key, shape, cuts, -0.22, 0.18)
    return jnp.clip(spiked(values, jax.random.fold_in(own_key, 3), *heavy), -bound, bound).astype(kind)


def setup_inputs(seed: int = 0) -> dict:
    key_list = jax.random.split(jax.random.key(seed), 8)
    return {
        "saved_input": draw_saved_input(jax.random.fold_in(key_list[7], 71), 0),
        "output_grad": bell_draw_with(key_list[1], (WORKERS, SEQ, D), 0.05, 0.3984375, ((0, 16), (1, 16)), (1, 2, 16, 2.0)),
        "weight_span": gaussian(key_list[2], (WORKERS, D, 3, FFC), D ** -0.5, 0.0625, ((0, 16), (1, 16))),
        "grad_carry": gaussian(key_list[3], (WORKERS, D, 3, FFC), 1.0, 6.0, ((0, 16), (1, 16)), jnp.float32),
        "attn_queries": draw_attn_queries(jax.random.fold_in(key_list[7], 71), 0),
        "attn_keys": draw_attn_keys(jax.random.fold_in(key_list[7], 71), 0),
        "attn_values": gaussian(key_list[6], (WORKERS, SEQ, KVH * HD), 1.0, 6.0, ((0, 16), (1, 16))),
    }


EPSILON = 1e-05
NEGATIVE = -1e+30

def matmul(left, right):
    return jnp.dot(left, right, preferred_element_type=jnp.float32)

def token_contract(left, right):
    return lax.dot_general(left, right, (((0,), (0,)), ((), ())), preferred_element_type=jnp.float32)

def normalize(activation):
    widened = activation.astype(jnp.float32)
    factor = lax.rsqrt(lax.optimization_barrier(jnp.mean(widened * widened, axis=-1, keepdims=True)) + EPSILON)
    return (widened * factor).astype(jnp.bfloat16)

def swiglu_back(gate_sum, up_sum, hidden_grad):
    sigmoid_gate = jax.nn.sigmoid(gate_sum)
    activated = gate_sum * sigmoid_gate
    hidden = (activated * up_sum).astype(jnp.bfloat16)
    up_grad = (hidden_grad * activated).astype(jnp.bfloat16)
    gate_grad = (hidden_grad * up_sum * sigmoid_gate * (1.0 + gate_sum * (1.0 - sigmoid_gate))).astype(jnp.bfloat16)
    return (hidden, gate_grad, up_grad)

def span_update(normed, cotangent, weights):
    gate_sum = matmul(normed, weights[:, 0])
    up_sum = matmul(normed, weights[:, 1])
    hidden_grad = matmul(cotangent, weights[:, 2])
    hidden, gate_grad, up_grad = swiglu_back(gate_sum, up_sum, hidden_grad)
    return jnp.stack([token_contract(normed, gate_grad), token_contract(normed, up_grad), token_contract(cotangent, hidden)], axis=1)

def attend_block(queries, keys_all, values_all, first_row, block_rows):
    group_size = QH // KVH
    query_block = lax.dynamic_slice_in_dim(queries, first_row, block_rows, 0)
    query_block = query_block.reshape(block_rows, KVH, group_size, HD).astype(jnp.float32)
    key_block = keys_all.reshape(SEQ, KVH, HD).astype(jnp.float32)
    value_block = values_all.reshape(SEQ, KVH, HD).astype(jnp.float32)
    scores = jnp.einsum('skgd,pkd->kgsp', query_block, key_block) * HD ** (-0.5)
    query_pos = first_row + jnp.arange(block_rows, dtype=jnp.int32)
    key_pos = jnp.arange(SEQ, dtype=jnp.int32)
    allowed = key_pos[None, :] <= query_pos[:, None]
    scores = jnp.where(allowed, scores, NEGATIVE)
    row_max = lax.optimization_barrier(jnp.max(scores, axis=-1, keepdims=True))
    probs = jnp.where(allowed, jnp.exp(scores - row_max), 0.0)
    denominators = lax.optimization_barrier(jnp.sum(probs, axis=-1))
    rounded_probs = lax.optimization_barrier(probs.astype(jnp.bfloat16)).astype(jnp.float32)
    numerator = jnp.einsum('kgsp,pkd->kgsd', rounded_probs, value_block)
    result = numerator / denominators[..., None]
    return jnp.transpose(result, (2, 0, 1, 3)).reshape(block_rows, QH * HD).astype(jnp.bfloat16)

def reference(saved_input, output_grad, weight_span, grad_carry, attn_queries, attn_keys, attn_values):
    arrived = jnp.roll(weight_span, 1, axis=0)
    onward = jnp.roll(grad_carry, -1, axis=0)

    def worker_update(worker):
        normed = normalize(saved_input[worker])
        return onward[worker] + span_update(normed, output_grad[worker], arrived[worker])
    carry_out = lax.map(worker_update, jnp.arange(WORKERS, dtype=jnp.int32))
    block_rows = math.gcd(SEQ, 256)

    def worker_attend(worker):
        queries = attn_queries[worker]
        keys_all = attn_keys[worker]
        values_all = attn_values[worker]
        starts = jnp.arange(SEQ // block_rows, dtype=jnp.int32) * block_rows
        blocks = lax.map(lambda first_row: attend_block(queries, keys_all, values_all, first_row, block_rows), starts)
        return blocks.reshape(SEQ, QH * HD)
    attn_out = lax.map(worker_attend, jnp.arange(WORKERS, dtype=jnp.int32))
    return (carry_out, attn_out)
```

```python
import jax
import jax.numpy as jnp
from jax import lax
from jax.sharding import Mesh, PartitionSpec as P

HD = 128
QH = 32
KVH = 4

EPSILON = 1e-05
NEGATIVE = -1e30


def shifted(block, axis, distance):
    devices = range(lax.axis_size(axis))
    route = [((i - distance) % len(devices), i) for i in devices]
    return lax.ppermute(block, axis, route)


def token_contract(left, right):
    return lax.dot_general(
        left, right, (((0,), (0,)), ((), ())), preferred_element_type=jnp.float32
    )


def matmul(left, right):
    return jnp.dot(left, right, preferred_element_type=jnp.float32)


def normalize(activation):
    widened = activation.astype(jnp.float32)
    factor = lax.rsqrt(jnp.mean(widened * widened, axis=-1, keepdims=True) + EPSILON)
    return (widened * factor).astype(jnp.bfloat16)


def swiglu_back(gate_sum, up_sum, hidden_grad):
    sigmoid_gate = jax.nn.sigmoid(gate_sum)
    activated = gate_sum * sigmoid_gate
    hidden = (activated * up_sum).astype(jnp.bfloat16)
    up_grad = (hidden_grad * activated).astype(jnp.bfloat16)
    gate_grad = (
        hidden_grad * up_sum * sigmoid_gate * (1.0 + gate_sum * (1.0 - sigmoid_gate))
    ).astype(jnp.bfloat16)
    return (hidden, gate_grad, up_grad)


def pair_split(block, side):
    rows, columns = block.shape
    halves = block.reshape(rows, 2, columns // 2)
    first = side == 0
    keep = jnp.where(first, halves[:, 0], halves[:, 1])
    give = jnp.where(first, halves[:, 1], halves[:, 0])
    return keep, give


def pair_rows(own, other, side):
    first = side == 0
    return jnp.concatenate([jnp.where(first, own, other), jnp.where(first, other, own)], axis=0)


def feature_split(block, side, layers):
    rows, columns = block.shape
    pieces = block.reshape(rows, layers, 2, columns // layers // 2)
    first = side == 0
    keep = jnp.where(first, pieces[:, :, 0], pieces[:, :, 1]).reshape(rows, columns // 2)
    give = jnp.where(first, pieces[:, :, 1], pieces[:, :, 0]).reshape(rows, columns // 2)
    return keep, give


def attend(queries, keys, values, first_row):
    rows, columns = queries.shape
    kv_heads = keys.shape[1] // HD
    group = columns // HD // kv_heads
    length = keys.shape[0]
    grouped = queries.reshape(rows, kv_heads, group, HD)
    query_pos = first_row + jnp.arange(rows, dtype=jnp.int32)
    running_max = jnp.full((kv_heads, group, rows), NEGATIVE, jnp.float32)
    running_sum = jnp.zeros((kv_heads, group, rows), jnp.float32)
    summed = jnp.zeros((kv_heads, group, rows, HD), jnp.float32)
    block_rows = min(512, length)
    for offset in range(0, length, block_rows):
        key_block = keys[offset : offset + block_rows].reshape(block_rows, kv_heads, HD)
        value_block = values[offset : offset + block_rows].reshape(block_rows, kv_heads, HD)
        scores = jnp.einsum(
            "skgd,pkd->kgsp", grouped, key_block, preferred_element_type=jnp.float32
        ) * HD ** (-0.5)
        key_pos = offset + jnp.arange(block_rows, dtype=jnp.int32)
        allowed = key_pos[None, :] <= query_pos[:, None]
        scores = jnp.where(allowed, scores, NEGATIVE)
        new_max = jnp.maximum(running_max, jnp.max(scores, axis=-1))
        probs = jnp.where(allowed, jnp.exp(scores - new_max[..., None]), 0.0)
        rescale = jnp.exp(running_max - new_max)
        running_sum = running_sum * rescale + jnp.sum(probs, axis=-1)
        summed = summed * rescale[..., None] + jnp.einsum(
            "kgsp,pkd->kgsd",
            probs.astype(jnp.bfloat16),
            value_block,
            preferred_element_type=jnp.float32,
        )
        running_max = new_max
    result = summed / running_sum[..., None]
    return jnp.transpose(result, (2, 0, 1, 3)).reshape(rows, columns).astype(jnp.bfloat16)


def shards(saved_input, output_grad, weight_span, grad_carry, attn_queries, attn_keys, attn_values):
    side = lax.axis_index("x")
    layer = lax.axis_index("z")
    layers = lax.axis_size("z")
    rows = saved_input.shape[1]

    key_keep, key_give = pair_split(attn_keys[0], side)
    value_keep, value_give = pair_split(attn_values[0], side)
    pair_keep = jnp.concatenate([key_keep, value_keep], axis=1)
    pair_give = jnp.concatenate([key_give, value_give], axis=1)
    pair_got = shifted(pair_give, "x", 1)
    arrived = shifted(jnp.transpose(weight_span[0], (1, 0, 2)), "blk", 1)
    keys_values = lax.all_gather(pair_rows(pair_keep, pair_got, side), "z", axis=0, tiled=True)
    weights = lax.all_gather(arrived, "z", axis=1, tiled=True)

    normed_keep, normed_give = feature_split(normalize(saved_input[0]), side, layers)
    grad_keep, grad_give = feature_split(output_grad[0], side, layers)
    normed = pair_rows(normed_keep, shifted(normed_give, "x", 1), side)
    cotangent = pair_rows(grad_keep, shifted(grad_give, "x", 1), side)

    query_keep, query_give = pair_split(attn_queries[0], side)
    queries = pair_rows(query_keep, shifted(query_give, "x", 1), side)
    carried = shifted(jnp.transpose(grad_carry[0], (1, 0, 2)).astype(jnp.bfloat16), "blk", -1)

    partial = jnp.stack(
        [matmul(normed, weights[0]), matmul(normed, weights[1]), matmul(cotangent, weights[2])]
    )
    sums = partial + shifted(partial.astype(jnp.bfloat16), "x", 1).astype(jnp.float32)
    hidden, gate_grad, up_grad = swiglu_back(sums[0], sums[1], sums[2])
    update = jnp.stack(
        [
            token_contract(normed, gate_grad),
            token_contract(normed, up_grad),
            token_contract(cotangent, hidden),
        ]
    ).astype(jnp.bfloat16)
    update = lax.psum_scatter(update, "z", scatter_dimension=1, tiled=True)
    carry_out = carried.astype(jnp.float32) + update.astype(jnp.float32)
    carry_out = jnp.transpose(carry_out, (1, 0, 2))[None]

    half = keys_values.shape[1] // 2
    both = attend(queries, keys_values[:, :half], keys_values[:, half:], layer * 2 * rows)
    first = side == 0
    mine = jnp.where(first, both[:rows], both[rows:])
    theirs = jnp.where(first, both[rows:], both[:rows])
    got = shifted(theirs, "x", 1)
    attn_out = jnp.concatenate([jnp.where(first, mine, got), jnp.where(first, got, mine)], axis=1)
    return (carry_out, attn_out[None])


def solution(mesh):
    workers, parts = mesh.devices.shape
    split = Mesh(mesh.devices.reshape(workers, parts // 2, 2), ("blk", "z", "x"))
    seq = ("z", "x")
    return jax.shard_map(
        shards,
        mesh=split,
        in_specs=(
            P("blk", seq, None),
            P("blk", seq, None),
            P("blk", seq, None, None),
            P("blk", seq, None, None),
            P("blk", seq, None),
            P("blk", seq, None),
            P("blk", seq, None),
        ),
        out_specs=(P("blk", seq, None, None), P("blk", seq, None)),
        check_vma=False,
    )
```

```python
import functools
import math

import jax
import jax.numpy as jnp
from jax import lax
from jax.experimental import pallas as pl
from jax.experimental.pallas import tpu as pltpu
from jax.sharding import Mesh, PartitionSpec as P

HD = 128
QH = 32
KVH = 4

EPSILON = 1e-05
NEGATIVE = -1e30


def shifted(block, axis, distance):
    devices = range(lax.axis_size(axis))
    route = [((i - distance) % len(devices), i) for i in devices]
    return lax.ppermute(block, axis, route)


def matmul(left, right):
    return jnp.dot(left, right, preferred_element_type=jnp.float32)


def swiglu_back(gate_sum, up_sum, hidden_grad):
    sigmoid_gate = jax.nn.sigmoid(gate_sum)
    activated = gate_sum * sigmoid_gate
    hidden = (activated * up_sum).astype(jnp.bfloat16)
    up_grad = (hidden_grad * activated).astype(jnp.bfloat16)
    gate_grad = (
        hidden_grad * up_sum * sigmoid_gate * (1.0 + gate_sum * (1.0 - sigmoid_gate))
    ).astype(jnp.bfloat16)
    return (hidden, gate_grad, up_grad)


def pair_split(block, side):
    rows, columns = block.shape
    low, high = block[:, : columns // 2], block[:, columns // 2 :]
    first = side == 0
    return jnp.where(first, low, high), jnp.where(first, high, low)


def pair_rows(own, other, side):
    first = side == 0
    return jnp.concatenate([jnp.where(first, own, other), jnp.where(first, other, own)], axis=0)


def tie(*arrays):
    return lax.optimization_barrier(arrays)


VMEM_BYTES = 40 * 1024 * 1024


def whole(count):
    return [pl.BlockSpec(memory_space=pltpu.VMEM)] * count


def split_kernel(layers, normalized, place, block, keep, give):
    layer, side = place[0], place[1]
    rows, columns = block.shape
    width = columns // layers // 2
    if normalized:
        total = jnp.zeros((rows, width), jnp.float32)
        for k in range(2 * layers):
            widened = block[:, k * width : (k + 1) * width].astype(jnp.float32)
            total = total + widened * widened
        factor = lax.rsqrt(jnp.sum(total, axis=1, keepdims=True) / columns + EPSILON)
    for j in range(layers):
        first = ((layer + j) % layers) * (2 * width)
        for out, which in ((keep, side), (give, 1 - side)):
            start = pl.multiple_of(first + which * width, width)
            piece = block[:, pl.ds(start, width)]
            if normalized:
                piece = (piece.astype(jnp.float32) * factor).astype(jnp.bfloat16)
            out[j] = piece


def feature_split(block, place, layers, normalized):
    rows, columns = block.shape
    shape = jax.ShapeDtypeStruct((layers, rows, columns // layers // 2), jnp.bfloat16)
    return pl.pallas_call(
        functools.partial(split_kernel, layers, normalized),
        in_specs=[pl.BlockSpec(memory_space=pltpu.SMEM)] + whole(1),
        out_specs=whole(2),
        out_shape=[shape, shape],
        cost_estimate=pl.CostEstimate(
            flops=4 * rows * columns, bytes_accessed=4 * rows * columns, transcendentals=0
        ),
        compiler_params=pltpu.CompilerParams(vmem_limit_bytes=VMEM_BYTES),
    )(place, block)


def partial_kernel(layers, keep, got, cot_keep, cot_got, *refs):
    weights, (exact, narrow) = refs[:-2], refs[-2:]
    half = layers // 2
    total = None
    for j in [0] + [k for step in range(1, half) for k in (step, layers - step)] + [half]:
        normed = jnp.concatenate([keep[j], got[j]], axis=0)
        cotangent = jnp.concatenate([cot_keep[j], cot_got[j]], axis=0)
        weight = weights[j][...]
        both = jnp.concatenate([weight[0], weight[1]], axis=1)
        term = jnp.concatenate([matmul(normed, both), matmul(cotangent, weight[2])], axis=1)
        total = term if total is None else total + term
    exact[...] = total
    narrow[...] = total.astype(jnp.bfloat16)


def partial_sums(pieces, weights):
    layers, rows, width = pieces[0].shape
    columns = 3 * weights[0].shape[2]
    return pl.pallas_call(
        functools.partial(partial_kernel, layers),
        in_specs=whole(4 + layers),
        out_specs=whole(2),
        out_shape=[
            jax.ShapeDtypeStruct((2 * rows, columns), jnp.float32),
            jax.ShapeDtypeStruct((2 * rows, columns), jnp.bfloat16),
        ],
        cost_estimate=pl.CostEstimate(
            flops=4 * layers * rows * width * columns,
            bytes_accessed=2 * layers * width * (4 * rows + columns),
            transcendentals=0,
        ),
        compiler_params=pltpu.CompilerParams(vmem_limit_bytes=VMEM_BYTES),
    )(*pieces, *weights)


def terms_kernel(partial, passed, keep, got, cot_keep, cot_got, own, *terms):
    rows = partial.shape[0] // 2
    half_f = partial.shape[1] // 3
    swapped = jnp.concatenate([passed[rows:], passed[:rows]], axis=0).astype(jnp.float32)
    sums = partial[...] + swapped
    hidden, gate_grad, up_grad = swiglu_back(
        sums[:, :half_f], sums[:, half_f : 2 * half_f], sums[:, 2 * half_f :]
    )
    grads = jnp.concatenate(
        [gate_grad.astype(jnp.float32).T, up_grad.astype(jnp.float32).T], axis=0
    ).astype(jnp.bfloat16)
    hidden = hidden.astype(jnp.float32).T.astype(jnp.bfloat16)
    for j, out in enumerate((own,) + terms):
        normed = jnp.concatenate([keep[j], got[j]], axis=0)
        cotangent = jnp.concatenate([cot_keep[j], cot_got[j]], axis=0)
        term = jnp.concatenate([matmul(grads, normed), matmul(hidden, cotangent)], axis=0)
        out[...] = term.astype(out.dtype)


def gradient_terms(partial, passed, pieces):
    layers, rows, width = pieces[0].shape
    columns = partial.shape[1]
    own = jax.ShapeDtypeStruct((columns, width), jnp.float32)
    term = jax.ShapeDtypeStruct((columns, width), jnp.bfloat16)
    return pl.pallas_call(
        terms_kernel,
        in_specs=whole(6),
        out_specs=whole(layers),
        out_shape=[own] + [term] * (layers - 1),
        cost_estimate=pl.CostEstimate(
            flops=4 * layers * rows * width * columns,
            bytes_accessed=layers * width * (8 * rows + 2 * columns),
            transcendentals=2 * rows * columns,
        ),
        compiler_params=pltpu.CompilerParams(vmem_limit_bytes=VMEM_BYTES),
    )(partial, passed, *pieces)


def gather_ring(block, layers, far, after=None):
    half = layers // 2
    up, down = block, block
    found = {0: block}
    for step in range(1, half):
        up, down = shifted(up, "z", 1), shifted(down, "z", -1)
        if after is not None:
            up, down = after(step, up, down)
        found[layers - step], found[step] = up, down
    found[half] = shifted(up, "z", 1) if far > 0 else shifted(down, "z", -1)
    return [found[j] for j in range(layers)]


def scatter_ring(terms, far):
    layers = len(terms)
    half = layers // 2
    routes = {1: list(range(half, 0, -1)), -1: list(range(half, layers))}
    routes[-far] = routes[-far][1:]
    sums = {1: None, -1: None}
    for step in range(half):
        for way in (1, -1):
            if step < len(routes[way]):
                term = terms[routes[way][step]]
                if sums[way] is not None:
                    term = term.astype(jnp.float32) + sums[way].astype(jnp.float32)
                sums[way] = shifted(term.astype(jnp.bfloat16), "z", way)
    return sums[1], sums[-1]


def close_kernel(carried, *refs):
    sums, out = refs[:-1], refs[-1]
    count = carried.shape[0]
    for which in range(len(sums) // 3):
        own, up, down = sums[3 * which : 3 * which + 3]
        total = own[...] + up[...].astype(jnp.float32) + down[...].astype(jnp.float32)
        half_f = total.shape[0] // count
        columns = slice(which * half_f, (which + 1) * half_f)
        for i in range(count):
            turned = total[i * half_f : (i + 1) * half_f].T
            out[i, :, columns] = carried[i, :, columns].astype(jnp.float32) + turned


def close(carried, sums):
    size = carried.size
    return pl.pallas_call(
        close_kernel,
        in_specs=whole(1 + len(sums)),
        out_specs=pl.BlockSpec(memory_space=pltpu.VMEM),
        out_shape=jax.ShapeDtypeStruct(carried.shape, jnp.float32),
        cost_estimate=pl.CostEstimate(flops=3 * size, bytes_accessed=14 * size, transcendentals=0),
        compiler_params=pltpu.CompilerParams(vmem_limit_bytes=VMEM_BYTES),
    )(carried, *sums)


def attend_kernel(layers, place, own, other, *refs):
    pieces, (mine, theirs) = refs[:layers], refs[layers:]
    rows = own.shape[0]
    layer, side = place[0], place[1]
    length = pieces[0].shape[0]
    exponent_scale = HD ** (-0.5) * math.log2(math.e)
    row = lax.broadcasted_iota(jnp.int32, (2 * rows, length), 0)
    column = lax.broadcasted_iota(jnp.int32, (2 * rows, length), 1)
    position = jnp.where(row < rows, row + side * rows, row - side * rows)
    diagonal = jnp.where(column <= position, 0.0, NEGATIVE)
    biases = [jnp.where(layer + j >= layers, 0.0, NEGATIVE) for j in range(1, layers)]

    def head(h, carry):
        columns = pl.ds(pl.multiple_of(h * HD, HD), HD)
        query = jnp.concatenate([own[:, columns], other[:, columns]], axis=0)
        scores = []
        for j, piece in enumerate(pieces):
            score = lax.dot_general(
                query, piece[:, :HD], (((1,), (1,)), ((), ())), preferred_element_type=jnp.float32
            )
            scores.append(score + (diagonal if j == 0 else biases[j - 1]))
        largest = functools.reduce(jnp.maximum, scores)
        largest = jnp.max(largest, axis=1, keepdims=True)
        total = jnp.zeros((2 * rows, length), jnp.float32)
        result = jnp.zeros((2 * rows, HD), jnp.float32)
        for score, piece in zip(scores, pieces):
            probs = jnp.exp2((score - largest) * exponent_scale)
            total = total + probs
            result = result + jnp.dot(
                probs.astype(jnp.bfloat16), piece[:, HD:], preferred_element_type=jnp.float32
            )
        result = (result / jnp.sum(total, axis=1, keepdims=True)).astype(jnp.bfloat16)
        mine[:, columns] = result[:rows]
        theirs[:, columns] = result[rows:]
        return carry

    lax.fori_loop(0, own.shape[1] // HD, head, 0)


def attend(own, other, pieces, place, part, parts):
    rows, columns = own.shape
    layers = len(pieces)
    length, width = pieces[0].shape
    kv_heads = width // 2 // HD
    share = columns // parts
    block = pl.BlockSpec((rows, share), lambda i: (0, part))
    out_block = pl.BlockSpec((rows, share), lambda i: (0, 0))
    kv_block = pl.BlockSpec((length, 2 * HD), lambda i: (0, part * kv_heads // parts))
    return pl.pallas_call(
        functools.partial(attend_kernel, layers),
        grid=(1,),
        in_specs=[pl.BlockSpec(memory_space=pltpu.SMEM), block, block] + [kv_block] * layers,
        out_specs=[out_block, out_block],
        out_shape=[jax.ShapeDtypeStruct((rows, share), jnp.bfloat16)] * 2,
        cost_estimate=pl.CostEstimate(
            flops=8 * rows * share * layers * length,
            bytes_accessed=8 * rows * share + 4 * layers * length * HD,
            transcendentals=2 * rows * share // HD * layers * length,
        ),
        compiler_params=pltpu.CompilerParams(vmem_limit_bytes=VMEM_BYTES),
    )(place, own, other, *pieces)


def shards(saved_input, output_grad, weight_span, grad_carry, attn_queries, attn_keys, attn_values):
    side = lax.axis_index("x")
    layer = lax.axis_index("z")
    layers = lax.axis_size("z")
    place = jnp.stack([layer, side]).astype(jnp.int32)
    half = layers // 2
    span = jnp.transpose(weight_span[0], (1, 0, 2))
    half_f = span.shape[2] // 2

    hops = tie(span[:, :, :half_f], span[:, :, half_f:], attn_keys, attn_values)
    hop0, hop1, attn_keys, attn_values = hops
    arrived = [shifted(hop0, "blk", 1), shifted(hop1, "blk", 1)]

    pair = jnp.concatenate(
        [
            array[0, :, k * HD : (k + 1) * HD]
            for k in range(KVH)
            for array in (attn_keys, attn_values)
        ],
        axis=1,
    )
    pair_keep, pair_give = pair_split(pair, side)
    pair_got = shifted(pair_give, "x", 1)
    token_rows = pair_rows(pair_keep, pair_got, side)

    saved_input, output_grad, token_rows = tie(saved_input, output_grad, token_rows)
    normed_keep, normed_give = feature_split(saved_input[0], place, layers, True)
    grad_keep, grad_give = feature_split(output_grad[0], place, layers, False)
    query_keep, query_give = pair_split(attn_queries[0], side)

    def ahead(step, up, down):
        nonlocal normed_give, grad_give
        if step == 1:
            up, down, arrived[0], normed_give, grad_give = tie(
                up, down, arrived[0], normed_give, grad_give
            )
        return up, down

    keys_values = gather_ring(token_rows, layers, -1, ahead)
    query_got = shifted(query_give, "x", 1)
    normed_got = shifted(normed_give, "x", 1)
    grad_got = shifted(grad_give, "x", 1)

    parts = layers // 2
    shares = []

    def share(*arrays):
        *arrays, queries = tie(*arrays, query_keep)
        part = len(shares)
        shares.append(list(attend(queries, query_got, keys_values, place, part, parts)))
        return arrays

    def shared(*arrays):
        *arrays, shares[-1][0] = tie(*arrays, shares[-1][0])
        return arrays

    def behind(step, up, down):
        if step == 2:
            up, down, arrived[1] = tie(up, down, arrived[1])
        return up, down

    def beside(step, up, down):
        if step > 1:
            up, down = shared(up, down)
        if step < 3:
            up, down = share(up, down)
        return up, down

    weights = [gather_ring(arrived[0], layers, 1, behind)]
    weights.append(gather_ring(arrived[1], layers, -1, beside))

    pieces = (normed_keep, normed_got, grad_keep, grad_got)
    exacts, passed = [], []
    for which in range(2):
        exact, narrow = partial_sums(pieces, weights[which])
        if which == 0:
            narrow, grad_carry = tie(narrow, grad_carry)
        if len(shares) < parts:
            exact, narrow = share(exact, narrow)
        exacts.append(exact)
        passed.append(*shared(shifted(narrow, "x", 1)))
    carried = shifted(jnp.transpose(grad_carry[0], (1, 0, 2)).astype(jnp.bfloat16), "blk", -1)

    outs = []
    for which in range(2):
        own, *terms = gradient_terms(exacts[which], passed[which], pieces)
        outs += [own, *scatter_ring([None] + terms, 1 - 2 * which)]
    carry_out = jnp.transpose(close(carried, outs), (1, 0, 2))[None]

    mine = jnp.concatenate([piece[0] for piece in shares], axis=1)
    got = shifted(jnp.concatenate([piece[1] for piece in shares], axis=1), "x", 1)
    first = side == 0
    attn_out = jnp.concatenate([jnp.where(first, mine, got), jnp.where(first, got, mine)], axis=1)
    return (carry_out, attn_out[None])


def solution(mesh):
    workers, parts = mesh.devices.shape
    split = Mesh(mesh.devices.reshape(workers, parts // 2, 2), ("blk", "z", "x"))
    seq = ("z", "x")
    return jax.shard_map(
        shards,
        mesh=split,
        in_specs=(
            P("blk", seq, None),
            P("blk", seq, None),
            P("blk", seq, None, None),
            P("blk", seq, None, None),
            P("blk", seq, None),
            P("blk", seq, None),
            P("blk", seq, None),
        ),
        out_specs=(P("blk", seq, None, None), P("blk", seq, None)),
        check_vma=False,
    )
```

```python
import functools
import math

import jax
import jax.numpy as jnp
from jax import lax
from jax.experimental import pallas as pl
from jax.experimental.pallas import tpu as pltpu
from jax.sharding import Mesh, PartitionSpec as P

HD = 128
QH = 32
KVH = 4

EPSILON = 1e-05
NEGATIVE = -1e30


def shifted(block, axis, distance):
    devices = range(lax.axis_size(axis))
    route = [((i - distance) % len(devices), i) for i in devices]
    return lax.ppermute(block, axis, route)


def matmul(left, right):
    return jnp.dot(left, right, preferred_element_type=jnp.float32)


def swiglu_back(gate_sum, up_sum, hidden_grad):
    sigmoid_gate = jax.nn.sigmoid(gate_sum)
    activated = gate_sum * sigmoid_gate
    hidden = (activated * up_sum).astype(jnp.bfloat16)
    up_grad = (hidden_grad * activated).astype(jnp.bfloat16)
    gate_grad = (
        hidden_grad * up_sum * sigmoid_gate * (1.0 + gate_sum * (1.0 - sigmoid_gate))
    ).astype(jnp.bfloat16)
    return (hidden, gate_grad, up_grad)


def pair_split(block, side):
    rows, columns = block.shape
    low, high = block[:, : columns // 2], block[:, columns // 2 :]
    first = side == 0
    return jnp.where(first, low, high), jnp.where(first, high, low)


def pair_rows(own, other, side):
    first = side == 0
    return jnp.concatenate([jnp.where(first, own, other), jnp.where(first, other, own)], axis=0)


def tie(*arrays):
    return lax.optimization_barrier(arrays)


VMEM_BYTES = 40 * 1024 * 1024


def whole(count):
    return [pl.BlockSpec(memory_space=pltpu.VMEM)] * count


def split_kernel(layers, normalized, place, block, keep, give):
    layer, side = place[0], place[1]
    rows, columns = block.shape
    width = columns // layers // 2
    if normalized:
        total = jnp.zeros((rows, width), jnp.float32)
        for k in range(2 * layers):
            widened = block[:, k * width : (k + 1) * width].astype(jnp.float32)
            total = total + widened * widened
        factor = lax.rsqrt(jnp.sum(total, axis=1, keepdims=True) / columns + EPSILON)
    for j in range(layers):
        first = ((layer + j) % layers) * (2 * width)
        for out, which in ((keep, side), (give, 1 - side)):
            start = pl.multiple_of(first + which * width, width)
            piece = block[:, pl.ds(start, width)]
            if normalized:
                piece = (piece.astype(jnp.float32) * factor).astype(jnp.bfloat16)
            out[j] = piece


def feature_split(block, place, layers, normalized):
    rows, columns = block.shape
    shape = jax.ShapeDtypeStruct((layers, rows, columns // layers // 2), jnp.bfloat16)
    return pl.pallas_call(
        functools.partial(split_kernel, layers, normalized),
        in_specs=[pl.BlockSpec(memory_space=pltpu.SMEM)] + whole(1),
        out_specs=whole(2),
        out_shape=[shape, shape],
        cost_estimate=pl.CostEstimate(
            flops=4 * rows * columns, bytes_accessed=4 * rows * columns, transcendentals=0
        ),
        compiler_params=pltpu.CompilerParams(vmem_limit_bytes=VMEM_BYTES),
    )(place, block)


def pair_piece(keep, got, j):
    return jnp.concatenate([keep[j], got[j]], axis=0)


def partial_kernel(layers, keep, got, cot_keep, cot_got, *refs):
    weights, (exact, narrow) = refs[:layers], refs[layers:]
    total = None
    for j, weight in enumerate(weights):
        both = jnp.concatenate([weight[0], weight[1]], axis=1)
        term = jnp.concatenate(
            [
                matmul(pair_piece(keep, got, j), both),
                matmul(pair_piece(cot_keep, cot_got, j), weight[2]),
            ],
            axis=1,
        )
        total = term if total is None else total + term
    exact[...] = total
    narrow[...] = total.astype(jnp.bfloat16)


def partial_sums(pieces, weights):
    layers, rows, width = pieces[0].shape
    columns = 3 * weights[0].shape[2]
    weight = pl.BlockSpec((3, *weights[0].shape[1:]), lambda i: (0, 0, 0))
    piece = pl.BlockSpec(pieces[0].shape, lambda i: (0, 0, 0))
    sums = pl.BlockSpec((2 * rows, columns), lambda i: (0, 0))
    return pl.pallas_call(
        functools.partial(partial_kernel, layers),
        grid=(1,),
        in_specs=[piece] * 4 + [weight] * layers,
        out_specs=[sums, sums],
        out_shape=[
            jax.ShapeDtypeStruct((2 * rows, columns), jnp.float32),
            jax.ShapeDtypeStruct((2 * rows, columns), jnp.bfloat16),
        ],
        cost_estimate=pl.CostEstimate(
            flops=4 * layers * rows * width * columns,
            bytes_accessed=2 * layers * width * (4 * rows + columns),
            transcendentals=0,
        ),
        compiler_params=pltpu.CompilerParams(vmem_limit_bytes=VMEM_BYTES),
    )(*pieces, *weights)


def terms_kernel(partial, passed, keep, got, cot_keep, cot_got, own, *terms):
    rows = partial.shape[0] // 2
    half_f = partial.shape[1] // 3
    swapped = jnp.concatenate([passed[rows:], passed[:rows]], axis=0).astype(jnp.float32)
    sums = partial[...] + swapped
    hidden, gate_grad, up_grad = swiglu_back(
        sums[:, :half_f], sums[:, half_f : 2 * half_f], sums[:, 2 * half_f :]
    )
    grads = jnp.concatenate(
        [gate_grad.astype(jnp.float32).T, up_grad.astype(jnp.float32).T], axis=0
    ).astype(jnp.bfloat16)
    hidden = hidden.astype(jnp.float32).T.astype(jnp.bfloat16)
    for j, out in enumerate((own,) + terms):
        normed = pair_piece(keep, got, j)
        cotangent = pair_piece(cot_keep, cot_got, j)
        term = jnp.concatenate([matmul(grads, normed), matmul(hidden, cotangent)], axis=0)
        out[...] = term.astype(out.dtype)


def gradient_terms(partial, passed, pieces):
    layers, rows, width = pieces[0].shape
    columns = partial.shape[1]
    own = jax.ShapeDtypeStruct((columns, width), jnp.float32)
    term = jax.ShapeDtypeStruct((columns, width), jnp.bfloat16)
    return pl.pallas_call(
        terms_kernel,
        in_specs=whole(6),
        out_specs=whole(layers),
        out_shape=[own] + [term] * (layers - 1),
        cost_estimate=pl.CostEstimate(
            flops=4 * layers * rows * width * columns,
            bytes_accessed=layers * width * (8 * rows + 2 * columns),
            transcendentals=2 * rows * columns,
        ),
        compiler_params=pltpu.CompilerParams(vmem_limit_bytes=VMEM_BYTES),
    )(partial, passed, *pieces)


class Ring:
    def __init__(self, up, down):
        self.ends = [up, down]

    def go(self):
        self.ends = [shifted(self.ends[0], "z", 1), shifted(self.ends[1], "z", -1)]
        return self.ends

    def tied(self, *arrays):
        together = tie(*self.ends, *arrays)
        self.ends = list(together[:2])
        return together[2:]


def scatter_ring(terms, far, after):
    layers = len(terms)
    half = layers // 2
    routes = {1: list(range(half, 0, -1)), -1: list(range(half, layers))}
    routes[-far] = routes[-far][1:]
    sums = {1: None, -1: None}
    for step in range(half):
        for way in (1, -1):
            if step < len(routes[way]):
                term = terms[routes[way][step]]
                if sums[way] is not None:
                    term = term.astype(jnp.float32) + sums[way].astype(jnp.float32)
                sums[way] = shifted(term.astype(jnp.bfloat16), "z", way)
        sums[1], sums[-1] = after(step, sums[1], sums[-1])
    return sums[1], sums[-1]


def close_kernel(carried, *refs):
    sums, out = refs[:-1], refs[-1]
    count = carried.shape[0]
    for which in range(len(sums) // 3):
        own, up, down = sums[3 * which : 3 * which + 3]
        total = own[...] + up[...].astype(jnp.float32) + down[...].astype(jnp.float32)
        half_f = total.shape[0] // count
        columns = slice(which * half_f, (which + 1) * half_f)
        for i in range(count):
            turned = total[i * half_f : (i + 1) * half_f].T
            out[i, :, columns] = carried[i, :, columns].astype(jnp.float32) + turned


def close(carried, sums):
    size = carried.size
    return pl.pallas_call(
        close_kernel,
        in_specs=whole(1 + len(sums)),
        out_specs=pl.BlockSpec(memory_space=pltpu.VMEM),
        out_shape=jax.ShapeDtypeStruct(carried.shape, jnp.float32),
        cost_estimate=pl.CostEstimate(flops=3 * size, bytes_accessed=14 * size, transcendentals=0),
        compiler_params=pltpu.CompilerParams(vmem_limit_bytes=VMEM_BYTES),
    )(carried, *sums)


def attend_kernel(layers, place, own, other, *refs):
    pieces, (mine, theirs) = refs[:layers], refs[layers:]
    rows = own.shape[0]
    layer, side = place[0], place[1]
    length = 2 * rows
    exponent_scale = HD ** (-0.5) * math.log2(math.e)
    row = lax.broadcasted_iota(jnp.int32, (2 * rows, length), 0)
    column = lax.broadcasted_iota(jnp.int32, (2 * rows, length), 1)
    position = jnp.where(row < rows, row + side * rows, row - side * rows)
    diagonal = jnp.where(column <= position, 0.0, NEGATIVE)
    biases = [jnp.where(layer + j >= layers, 0.0, NEGATIVE) for j in range(1, layers)]

    def head(h, carry):
        columns = pl.ds(pl.multiple_of(h * HD, HD), HD)
        query = jnp.concatenate([own[:, columns], other[:, columns]], axis=0)
        scores = []
        for j, piece in enumerate(pieces):
            score = lax.dot_general(
                query, piece[0, :length], (((1,), (1,)), ((), ())), preferred_element_type=jnp.float32
            )
            scores.append(score + (diagonal if j == 0 else biases[j - 1]))
        largest = functools.reduce(jnp.maximum, scores)
        largest = jnp.max(largest, axis=1, keepdims=True)
        total = jnp.zeros((2 * rows, length), jnp.float32)
        result = jnp.zeros((2 * rows, HD), jnp.float32)
        for score, piece in zip(scores, pieces):
            probs = jnp.exp2((score - largest) * exponent_scale)
            total = total + probs
            result = result + jnp.dot(
                probs.astype(jnp.bfloat16), piece[0, length:], preferred_element_type=jnp.float32
            )
        result = (result / jnp.sum(total, axis=1, keepdims=True)).astype(jnp.bfloat16)
        mine[:, columns] = result[:rows]
        theirs[:, columns] = result[rows:]
        return carry

    lax.fori_loop(0, own.shape[1] // HD, head, 0)


def attend(own, other, pieces, place, part, parts):
    rows, columns = own.shape
    layers = len(pieces)
    share = columns // parts
    block = pl.BlockSpec((rows, share), lambda i: (0, part))
    out_block = pl.BlockSpec((rows, share), lambda i: (0, 0))
    kv_blocks = [
        pl.BlockSpec(
            (1, *piece.shape[1:]),
            lambda i, last=piece.shape[0] - 1: (last, 0, 0),
        )
        for piece in pieces
    ]
    length = 2 * rows
    return pl.pallas_call(
        functools.partial(attend_kernel, layers),
        grid=(1,),
        in_specs=[pl.BlockSpec(memory_space=pltpu.SMEM), block, block] + kv_blocks,
        out_specs=[out_block, out_block],
        out_shape=[jax.ShapeDtypeStruct((rows, share), jnp.bfloat16)] * 2,
        cost_estimate=pl.CostEstimate(
            flops=8 * rows * share * layers * length,
            bytes_accessed=8 * rows * share + 4 * layers * length * HD,
            transcendentals=2 * rows * share // HD * layers * length,
        ),
        compiler_params=pltpu.CompilerParams(vmem_limit_bytes=VMEM_BYTES),
    )(place, own, other, *pieces)


def shards(saved_input, output_grad, weight_span, grad_carry, attn_queries, attn_keys, attn_values):
    side = lax.axis_index("x")
    layer = lax.axis_index("z")
    layers = lax.axis_size("z")
    place = jnp.stack([layer, side]).astype(jnp.int32)

    def stacked(low):
        return [
            jnp.stack([array[0, :, k * HD : (k + 1) * HD] for array in (attn_keys, attn_values)])
            for k in range(low, low + KVH // 2)
        ]

    lower, upper = jnp.stack(stacked(0)), jnp.stack(stacked(KVH // 2))
    low = side == 0
    pair_keep, pair_give = jnp.where(low, lower, upper), jnp.where(low, upper, lower)
    pair_got = shifted(pair_give, "x", 1)

    span = jnp.transpose(weight_span[0], (1, 0, 2))
    half_f = span.shape[2] // 2
    hop0 = span[:, :, :half_f]
    span, hop0 = tie(span, hop0)
    arrived = [shifted(hop0, "blk", 1), shifted(span[:, :, half_f:], "blk", 1)]
    tokens = jnp.concatenate(
        [jnp.where(low, pair_keep, pair_got), jnp.where(low, pair_got, pair_keep)], axis=2
    )
    tokens = tokens.reshape(KVH // 2, -1, HD)
    query_keep, query_give = pair_split(attn_queries[0], side)
    saved_input, output_grad, tokens, query_give = tie(saved_input, output_grad, tokens, query_give)
    query_got = shifted(query_give, "x", 1)
    normed_keep, normed_give = feature_split(saved_input[0], place, layers, True)
    grad_keep, grad_give = feature_split(output_grad[0], place, layers, False)

    shares = []

    def share(*arrays):
        *arrays, queries = tie(*arrays, query_keep)
        head = heads[len(shares) // 2]
        pieces = [head[j] for j in range(layers)]
        mine, theirs = attend(queries, query_got, pieces, place, len(shares), 4)
        shares.append([mine, theirs])
        return arrays

    def kept(ring, found, step):
        found[layers - step], found[step] = ring.go()

    steps = layers // 2
    heads = [{0: tokens}, None]
    ring = Ring(tokens, tokens)
    kept(ring, heads[0], 1)
    arrived = list(ring.tied(*arrived))
    heads = [{j: heads[0][j][k : k + 1] for j in heads[0]} for k in range(2)]
    halves = [{0: arrived[0]}, {0: arrived[1]}]
    rings = [
        Ring(*[jnp.concatenate([arrived[k], end[k : k + 1]]) for end in ring.ends])
        for k in range(2)
    ]
    for step in range(1, steps):
        for k in range(2):
            kept(rings[k], halves[k], step)
            heads[k][layers - step - 1], heads[k][step + 1] = (
                halves[k][layers - step], halves[k][step]
            )
            if k == 0 and step == 1:
                (normed_give,) = rings[0].tied(normed_give)
                normed_got = shifted(normed_give, "x", 1)
            elif k == 0 and step == 2:
                (grad_give,) = rings[0].tied(grad_give)
                grad_got = shifted(grad_give, "x", 1)
            elif k == 0:
                (grad_carry,) = rings[0].tied(grad_carry)
            elif step == 1:
                (query_got,) = rings[1].tied(query_got)
            elif step == 2:
                (normed_got,) = rings[1].tied(normed_got)
            else:
                (grad_got,) = rings[1].tied(grad_got)
    carried = shifted(jnp.transpose(grad_carry[0], (1, 0, 2)).astype(jnp.bfloat16), "blk", -1)
    halves[0][steps] = shifted(rings[0].ends[0][:3], "z", 1)
    halves[1][steps] = shifted(rings[1].ends[1][:3], "z", -1)

    pieces = (normed_keep, normed_got, grad_keep, grad_got)
    exacts, passed = [], []
    for found in halves:
        exact, narrow = partial_sums(pieces, [found[j] for j in range(layers)])
        exacts.append(exact)
        (narrow,) = share(narrow)
        got, shares[-1][0] = tie(shifted(narrow, "x", 1), shares[-1][0])
        passed.append(got)
    passed[1], carried = tie(passed[1], carried)

    def plain(step, *arrays):
        return arrays

    def after(step, *arrays):
        if step in (1, 2):
            *arrays, shares[-1][0] = tie(*arrays, shares[-1][0])
        if step in (0, 1):
            arrays = share(*arrays)
        return arrays

    outs = []
    for which in range(2):
        own, *terms = gradient_terms(exacts[which], passed[which], pieces)
        outs += [own, *scatter_ring([None] + terms, 1 - 2 * which, after if which == 1 else plain)]
    carry_out = jnp.transpose(close(carried, outs), (1, 0, 2))[None]

    mine = jnp.concatenate([piece[0] for piece in shares], axis=1)
    got = shifted(jnp.concatenate([piece[1] for piece in shares], axis=1), "x", 1)
    attn_out = jnp.concatenate([jnp.where(low, mine, got), jnp.where(low, got, mine)], axis=1)
    return (carry_out, attn_out[None])


def solution(mesh):
    workers, parts = mesh.devices.shape
    split = Mesh(mesh.devices.reshape(workers, parts // 2, 2), ("blk", "z", "x"))
    seq = ("z", "x")
    return jax.shard_map(
        shards,
        mesh=split,
        in_specs=(
            P("blk", seq, None),
            P("blk", seq, None),
            P("blk", seq, None, None),
            P("blk", seq, None, None),
            P("blk", seq, None),
            P("blk", seq, None),
            P("blk", seq, None),
        ),
        out_specs=(P("blk", seq, None, None), P("blk", seq, None)),
        check_vma=False,
    )
```

```python
import functools
import math

import jax
import jax.numpy as jnp
from jax import lax
from jax.experimental import pallas as pl
from jax.experimental.pallas import tpu as pltpu
from jax.sharding import Mesh, PartitionSpec as P

HD = 128
QH = 32
KVH = 4

EPSILON = 1e-05
NEGATIVE = -1e30


def shifted(block, axis, distance):
    devices = range(lax.axis_size(axis))
    route = [((i - distance) % len(devices), i) for i in devices]
    return lax.ppermute(block, axis, route)


def matmul(left, right):
    return jnp.dot(left, right, preferred_element_type=jnp.float32)


def swiglu_back(gate_sum, up_sum, hidden_grad):
    sigmoid_gate = jax.nn.sigmoid(gate_sum)
    activated = gate_sum * sigmoid_gate
    hidden = (activated * up_sum).astype(jnp.bfloat16)
    up_grad = (hidden_grad * activated).astype(jnp.bfloat16)
    gate_grad = (
        hidden_grad * up_sum * sigmoid_gate * (1.0 + gate_sum * (1.0 - sigmoid_gate))
    ).astype(jnp.bfloat16)
    return (hidden, gate_grad, up_grad)


def pair_split(block, side):
    rows, columns = block.shape
    low, high = block[:, : columns // 2], block[:, columns // 2 :]
    first = side == 0
    return jnp.where(first, low, high), jnp.where(first, high, low)


def pair_rows(own, other, side):
    first = side == 0
    return jnp.concatenate([jnp.where(first, own, other), jnp.where(first, other, own)], axis=0)


def tie(*arrays):
    return lax.optimization_barrier(arrays)


VMEM_BYTES = 40 * 1024 * 1024


def whole(count):
    return [pl.BlockSpec(memory_space=pltpu.VMEM)] * count


def split_kernel(layers, normalized, place, block, keep, give):
    layer, side = place[0], place[1]
    rows, columns = block.shape
    width = columns // layers // 2
    if normalized:
        total = jnp.zeros((rows, width), jnp.float32)
        for k in range(2 * layers):
            widened = block[:, k * width : (k + 1) * width].astype(jnp.float32)
            total = total + widened * widened
        factor = lax.rsqrt(jnp.sum(total, axis=1, keepdims=True) / columns + EPSILON)
    for j in range(layers):
        first = ((layer + j) % layers) * (2 * width)
        for out, which in ((keep, side), (give, 1 - side)):
            start = pl.multiple_of(first + which * width, width)
            piece = block[:, pl.ds(start, width)]
            if normalized:
                piece = (piece.astype(jnp.float32) * factor).astype(jnp.bfloat16)
            out[j] = piece


def feature_split(block, place, layers, normalized):
    rows, columns = block.shape
    shape = jax.ShapeDtypeStruct((layers, rows, columns // layers // 2), jnp.bfloat16)
    return pl.pallas_call(
        functools.partial(split_kernel, layers, normalized),
        in_specs=[pl.BlockSpec(memory_space=pltpu.SMEM)] + whole(1),
        out_specs=whole(2),
        out_shape=[shape, shape],
        cost_estimate=pl.CostEstimate(
            flops=4 * rows * columns, bytes_accessed=4 * rows * columns, transcendentals=0
        ),
        compiler_params=pltpu.CompilerParams(vmem_limit_bytes=VMEM_BYTES),
    )(place, block)


def pair_piece(keep, got, j):
    return jnp.concatenate([keep[j], got[j]], axis=0)


def partial_kernel(layers, keep, got, cot_keep, cot_got, *refs):
    weights, (exact, narrow) = refs[:layers], refs[layers:]
    total = None
    for j, weight in enumerate(weights):
        both = jnp.concatenate([weight[0], weight[1]], axis=1)
        term = jnp.concatenate(
            [
                matmul(pair_piece(keep, got, j), both),
                matmul(pair_piece(cot_keep, cot_got, j), weight[2]),
            ],
            axis=1,
        )
        total = term if total is None else total + term
    exact[...] = total
    narrow[...] = total.astype(jnp.bfloat16)


def partial_sums(pieces, weights):
    layers, rows, width = pieces[0].shape
    columns = 3 * weights[0].shape[2]
    weight = pl.BlockSpec((3, *weights[0].shape[1:]), lambda i: (0, 0, 0))
    piece = pl.BlockSpec(pieces[0].shape, lambda i: (0, 0, 0))
    sums = pl.BlockSpec((2 * rows, columns), lambda i: (0, 0))
    return pl.pallas_call(
        functools.partial(partial_kernel, layers),
        grid=(1,),
        in_specs=[piece] * 4 + [weight] * layers,
        out_specs=[sums, sums],
        out_shape=[
            jax.ShapeDtypeStruct((2 * rows, columns), jnp.float32),
            jax.ShapeDtypeStruct((2 * rows, columns), jnp.bfloat16),
        ],
        cost_estimate=pl.CostEstimate(
            flops=4 * layers * rows * width * columns,
            bytes_accessed=2 * layers * width * (4 * rows + columns),
            transcendentals=0,
        ),
        compiler_params=pltpu.CompilerParams(vmem_limit_bytes=VMEM_BYTES),
    )(*pieces, *weights)


def terms_kernel(partial, passed, keep, got, cot_keep, cot_got, own, *terms):
    rows = partial.shape[0] // 2
    half_f = partial.shape[1] // 3
    swapped = jnp.concatenate([passed[rows:], passed[:rows]], axis=0).astype(jnp.float32)
    sums = partial[...] + swapped
    hidden, gate_grad, up_grad = swiglu_back(
        sums[:, :half_f], sums[:, half_f : 2 * half_f], sums[:, 2 * half_f :]
    )
    grads = jnp.concatenate(
        [gate_grad.astype(jnp.float32).T, up_grad.astype(jnp.float32).T], axis=0
    ).astype(jnp.bfloat16)
    hidden = hidden.astype(jnp.float32).T.astype(jnp.bfloat16)
    for j, out in enumerate((own,) + terms):
        normed = pair_piece(keep, got, j)
        cotangent = pair_piece(cot_keep, cot_got, j)
        term = jnp.concatenate([matmul(grads, normed), matmul(hidden, cotangent)], axis=0)
        out[...] = term.astype(out.dtype)


def gradient_terms(partial, passed, pieces):
    layers, rows, width = pieces[0].shape
    columns = partial.shape[1]
    own = jax.ShapeDtypeStruct((columns, width), jnp.float32)
    term = jax.ShapeDtypeStruct((columns, width), jnp.bfloat16)
    return pl.pallas_call(
        terms_kernel,
        in_specs=whole(6),
        out_specs=whole(layers),
        out_shape=[own] + [term] * (layers - 1),
        cost_estimate=pl.CostEstimate(
            flops=4 * layers * rows * width * columns,
            bytes_accessed=layers * width * (8 * rows + 2 * columns),
            transcendentals=2 * rows * columns,
        ),
        compiler_params=pltpu.CompilerParams(vmem_limit_bytes=VMEM_BYTES),
    )(partial, passed, *pieces)


class Ring:
    def __init__(self, up, down):
        self.ends = [up, down]

    def go(self):
        self.ends = [shifted(self.ends[0], "z", 1), shifted(self.ends[1], "z", -1)]
        return self.ends

    def tied(self, *arrays):
        together = tie(*self.ends, *arrays)
        self.ends = list(together[:2])
        return together[2:]


def scatter_ring(terms, far, after):
    layers = len(terms)
    half = layers // 2
    routes = {1: list(range(half, 0, -1)), -1: list(range(half, layers))}
    routes[-far] = routes[-far][1:]
    sums = {1: None, -1: None}
    for step in range(half):
        for way in (1, -1):
            if step < len(routes[way]):
                term = terms[routes[way][step]]
                if sums[way] is not None:
                    term = term.astype(jnp.float32) + sums[way].astype(jnp.float32)
                sums[way] = shifted(term.astype(jnp.bfloat16), "z", way)
        sums[1], sums[-1] = after(step, sums[1], sums[-1])
    return sums[1], sums[-1]


def close_kernel(carried, *refs):
    sums, out = refs[:-1], refs[-1]
    count = carried.shape[0]
    for which in range(len(sums) // 3):
        own, up, down = sums[3 * which : 3 * which + 3]
        total = own[...] + up[...].astype(jnp.float32) + down[...].astype(jnp.float32)
        half_f = total.shape[0] // count
        columns = slice(which * half_f, (which + 1) * half_f)
        for i in range(count):
            turned = total[i * half_f : (i + 1) * half_f].T
            out[i, :, columns] = carried[i, :, columns].astype(jnp.float32) + turned


def close(carried, sums):
    size = carried.size
    return pl.pallas_call(
        close_kernel,
        in_specs=whole(1 + len(sums)),
        out_specs=pl.BlockSpec(memory_space=pltpu.VMEM),
        out_shape=jax.ShapeDtypeStruct(carried.shape, jnp.float32),
        cost_estimate=pl.CostEstimate(flops=3 * size, bytes_accessed=14 * size, transcendentals=0),
        compiler_params=pltpu.CompilerParams(vmem_limit_bytes=VMEM_BYTES),
    )(carried, *sums)


def attend_kernel(layers, place, own, other, *refs):
    pieces, (mine, theirs) = refs[:layers], refs[layers:]
    rows = own.shape[0]
    layer, side = place[0], place[1]
    length = 2 * rows
    exponent_scale = HD ** (-0.5) * math.log2(math.e)
    row = lax.broadcasted_iota(jnp.int32, (2 * rows, length), 0)
    column = lax.broadcasted_iota(jnp.int32, (2 * rows, length), 1)
    position = jnp.where(row < rows, row + side * rows, row - side * rows)
    diagonal = jnp.where(column <= position, 0.0, NEGATIVE)
    biases = [jnp.where(layer + j >= layers, 0.0, NEGATIVE) for j in range(1, layers)]

    def head(h, carry):
        columns = pl.ds(pl.multiple_of(h * HD, HD), HD)
        query = jnp.concatenate([own[:, columns], other[:, columns]], axis=0)
        scores = []
        for j, piece in enumerate(pieces):
            score = lax.dot_general(
                query, piece[0, :length], (((1,), (1,)), ((), ())), preferred_element_type=jnp.float32
            )
            scores.append(score + (diagonal if j == 0 else biases[j - 1]))
        largest = functools.reduce(jnp.maximum, scores)
        largest = jnp.max(largest, axis=1, keepdims=True)
        total = jnp.zeros((2 * rows, length), jnp.float32)
        result = jnp.zeros((2 * rows, HD), jnp.float32)
        for score, piece in zip(scores, pieces):
            probs = jnp.exp2((score - largest) * exponent_scale)
            total = total + probs
            result = result + jnp.dot(
                probs.astype(jnp.bfloat16), piece[0, length:], preferred_element_type=jnp.float32
            )
        result = (result / jnp.sum(total, axis=1, keepdims=True)).astype(jnp.bfloat16)
        mine[:, columns] = result[:rows]
        theirs[:, columns] = result[rows:]
        return carry

    lax.fori_loop(0, own.shape[1] // HD, head, 0, unroll=4)


def attend(own, other, pieces, place, part, parts):
    rows, columns = own.shape
    layers = len(pieces)
    share = columns // parts
    block = pl.BlockSpec((rows, share), lambda i: (0, part))
    out_block = pl.BlockSpec((rows, share), lambda i: (0, 0))
    kv_blocks = [
        pl.BlockSpec(
            (1, *piece.shape[1:]),
            lambda i, last=piece.shape[0] - 1: (last, 0, 0),
        )
        for piece in pieces
    ]
    length = 2 * rows
    return pl.pallas_call(
        functools.partial(attend_kernel, layers),
        grid=(1,),
        in_specs=[pl.BlockSpec(memory_space=pltpu.SMEM), block, block] + kv_blocks,
        out_specs=[out_block, out_block],
        out_shape=[jax.ShapeDtypeStruct((rows, share), jnp.bfloat16)] * 2,
        cost_estimate=pl.CostEstimate(
            flops=8 * rows * share * layers * length,
            bytes_accessed=8 * rows * share + 4 * layers * length * HD,
            transcendentals=2 * rows * share // HD * layers * length,
        ),
        compiler_params=pltpu.CompilerParams(vmem_limit_bytes=VMEM_BYTES),
    )(place, own, other, *pieces)


def shards(saved_input, output_grad, weight_span, grad_carry, attn_queries, attn_keys, attn_values):
    side = lax.axis_index("x")
    layer = lax.axis_index("z")
    layers = lax.axis_size("z")
    place = jnp.stack([layer, side]).astype(jnp.int32)

    span = jnp.transpose(weight_span[0], (1, 0, 2))
    half_f = span.shape[2] // 2
    hop0 = span[:, :, :half_f]
    span, hop0 = tie(span, hop0)
    hop1 = span[:, :, half_f:]
    hop0, hop1, attn_keys, attn_values = tie(hop0, hop1, attn_keys, attn_values)
    arrived = [shifted(hop0, "blk", 1), shifted(hop1, "blk", 1)]

    def stacked(low):
        return [
            jnp.stack([array[0, :, k * HD : (k + 1) * HD] for array in (attn_keys, attn_values)])
            for k in range(low, low + KVH // 2)
        ]

    lower, upper = jnp.stack(stacked(0)), jnp.stack(stacked(KVH // 2))
    low = side == 0
    pair_keep, pair_give = jnp.where(low, lower, upper), jnp.where(low, upper, lower)
    pair_got = shifted(pair_give, "x", 1)

    tokens = jnp.concatenate(
        [jnp.where(low, pair_keep, pair_got), jnp.where(low, pair_got, pair_keep)], axis=2
    )
    tokens = tokens.reshape(KVH // 2, -1, HD)
    query_keep, query_give = pair_split(attn_queries[0], side)
    saved_input, output_grad, tokens = tie(saved_input, output_grad, tokens)
    arrived[1], query_give = tie(arrived[1], query_give)
    query_got = shifted(query_give, "x", 1)
    normed_keep, normed_give = feature_split(saved_input[0], place, layers, True)
    grad_keep, grad_give = feature_split(output_grad[0], place, layers, False)

    shares = []

    def share(*arrays):
        *arrays, queries = tie(*arrays, query_keep)
        head = heads[len(shares) // 2]
        pieces = [head[j] for j in range(layers)]
        mine, theirs = attend(queries, query_got, pieces, place, len(shares), 4)
        shares.append([mine, theirs])
        return arrays

    def kept(ring, found, step):
        found[layers - step], found[step] = ring.go()

    steps = layers // 2
    heads = [{0: tokens[k : k + 1]} for k in range(2)]
    arrived[0], tokens = tie(arrived[0], tokens)
    halves = [{0: part} for part in arrived]
    blocks = [jnp.concatenate([arrived[k], tokens[k : k + 1]]) for k in range(2)]
    rings = [Ring(block, block) for block in blocks]
    for step in range(1, steps):
        for k in range(2):
            kept(rings[k], halves[k], step)
            heads[k][layers - step], heads[k][step] = halves[k][layers - step], halves[k][step]
            if k == 0 and step == 1:
                (normed_give,) = rings[0].tied(normed_give)
                normed_got = shifted(normed_give, "x", 1)
            elif k == 0 and step == 2:
                (grad_give,) = rings[0].tied(grad_give)
                grad_got = shifted(grad_give, "x", 1)
            elif k == 1 and step == 1:
                (query_got,) = rings[1].tied(query_got)
            elif k == 1 and step == 2:
                (normed_got,) = rings[1].tied(normed_got)
            elif k == 1:
                (grad_got,) = rings[1].tied(grad_got)
    halves[0][steps] = heads[0][steps] = shifted(rings[0].ends[0], "z", 1)
    halves[1][steps] = heads[1][steps] = shifted(rings[1].ends[1], "z", -1)

    pieces = (normed_keep, normed_got, grad_keep, grad_got)
    exacts, passed = [], []
    for found in halves:
        exact, narrow = partial_sums(pieces, [found[j] for j in range(layers)])
        exacts.append(exact)
        (narrow,) = share(narrow)
        got, shares[-1][0] = tie(shifted(narrow, "x", 1), shares[-1][0])
        passed.append(got)
    passed[1], grad_carry = tie(passed[1], grad_carry)
    carried = [shifted(jnp.transpose(grad_carry[0], (1, 0, 2)).astype(jnp.bfloat16), "blk", -1)]

    def plain(step, *arrays):
        return arrays

    def after(step, *arrays):
        if step == 1:
            *arrays, carried[0] = tie(*arrays, carried[0])
        if step in (1, 2):
            *arrays, shares[-1][0] = tie(*arrays, shares[-1][0])
        if step in (0, 1):
            arrays = share(*arrays)
        return arrays

    outs = []
    for which in range(2):
        own, *terms = gradient_terms(exacts[which], passed[which], pieces)
        outs += [own, *scatter_ring([None] + terms, 1 - 2 * which, after if which == 1 else plain)]
    carry_out = jnp.transpose(close(carried[0], outs), (1, 0, 2))[None]

    mine = jnp.concatenate([piece[0] for piece in shares], axis=1)
    got = shifted(jnp.concatenate([piece[1] for piece in shares], axis=1), "x", 1)
    attn_out = jnp.concatenate([jnp.where(low, mine, got), jnp.where(low, got, mine)], axis=1)
    return (carry_out, attn_out[None])


def solution(mesh):
    workers, parts = mesh.devices.shape
    split = Mesh(mesh.devices.reshape(workers, parts // 2, 2), ("blk", "z", "x"))
    seq = ("z", "x")
    return jax.shard_map(
        shards,
        mesh=split,
        in_specs=(
            P("blk", seq, None),
            P("blk", seq, None),
            P("blk", seq, None, None),
            P("blk", seq, None, None),
            P("blk", seq, None),
            P("blk", seq, None),
            P("blk", seq, None),
        ),
        out_specs=(P("blk", seq, None, None), P("blk", seq, None)),
        check_vma=False,
    )
```

```python
import functools
import math

import jax
import jax.numpy as jnp
from jax import lax
from jax.experimental import pallas as pl
from jax.experimental.pallas import tpu as pltpu
from jax.sharding import Mesh, PartitionSpec as P

HD = 128
QH = 32
KVH = 4

EPSILON = 1e-05
NEGATIVE = -1e30


def shifted(block, axis, distance):
    devices = range(lax.axis_size(axis))
    route = [((i - distance) % len(devices), i) for i in devices]
    return lax.ppermute(block, axis, route)


def matmul(left, right):
    return jnp.dot(left, right, preferred_element_type=jnp.float32)


def swiglu_back(gate_sum, up_sum, hidden_grad):
    sigmoid_gate = jax.nn.sigmoid(gate_sum)
    activated = gate_sum * sigmoid_gate
    hidden = (activated * up_sum).astype(jnp.bfloat16)
    up_grad = (hidden_grad * activated).astype(jnp.bfloat16)
    gate_grad = (
        hidden_grad * up_sum * sigmoid_gate * (1.0 + gate_sum * (1.0 - sigmoid_gate))
    ).astype(jnp.bfloat16)
    return (hidden, gate_grad, up_grad)


def pair_split(block, side):
    rows, columns = block.shape
    low, high = block[:, : columns // 2], block[:, columns // 2 :]
    first = side == 0
    return jnp.where(first, low, high), jnp.where(first, high, low)


def pair_rows(own, other, side):
    first = side == 0
    return jnp.concatenate([jnp.where(first, own, other), jnp.where(first, other, own)], axis=0)


def tie(*arrays):
    return lax.optimization_barrier(arrays)


VMEM_BYTES = 40 * 1024 * 1024


def whole(count):
    return [pl.BlockSpec(memory_space=pltpu.VMEM)] * count


def cut_kernel(span, low, high, arrivals):
    half = low.shape[2]
    copies = [
        pltpu.make_async_copy(span.at[:, :, k * half : (k + 1) * half], out, arrivals.at[k])
        for k, out in enumerate((low, high))
    ]
    for copy in copies:
        copy.start()
    for copy in copies:
        copy.wait()


def cut(span):
    half = jax.ShapeDtypeStruct((*span.shape[:2], span.shape[2] // 2), span.dtype)
    anywhere = pl.BlockSpec(memory_space=pl.ANY)
    return pl.pallas_call(
        cut_kernel,
        in_specs=[anywhere],
        out_specs=[anywhere, anywhere],
        out_shape=[half, half],
        scratch_shapes=[pltpu.SemaphoreType.DMA((2,))],
        cost_estimate=pl.CostEstimate(flops=0, bytes_accessed=4 * span.size, transcendentals=0),
        compiler_params=pltpu.CompilerParams(vmem_limit_bytes=VMEM_BYTES),
    )(span)


def split_kernel(layers, normalized, place, block, keep, give):
    layer, side = place[0], place[1]
    rows, columns = block.shape
    width = columns // layers // 2
    if normalized:
        total = jnp.zeros((rows, width), jnp.float32)
        for k in range(2 * layers):
            widened = block[:, k * width : (k + 1) * width].astype(jnp.float32)
            total = total + widened * widened
        factor = lax.rsqrt(jnp.sum(total, axis=1, keepdims=True) / columns + EPSILON)
    for j in range(layers):
        first = ((layer + j) % layers) * (2 * width)
        for out, which in ((keep, side), (give, 1 - side)):
            start = pl.multiple_of(first + which * width, width)
            piece = block[:, pl.ds(start, width)]
            if normalized:
                piece = (piece.astype(jnp.float32) * factor).astype(jnp.bfloat16)
            out[j] = piece


def feature_split(block, place, layers, normalized):
    rows, columns = block.shape
    shape = jax.ShapeDtypeStruct((layers, rows, columns // layers // 2), jnp.bfloat16)
    return pl.pallas_call(
        functools.partial(split_kernel, layers, normalized),
        in_specs=[pl.BlockSpec(memory_space=pltpu.SMEM)] + whole(1),
        out_specs=whole(2),
        out_shape=[shape, shape],
        cost_estimate=pl.CostEstimate(
            flops=4 * rows * columns, bytes_accessed=4 * rows * columns, transcendentals=0
        ),
        compiler_params=pltpu.CompilerParams(vmem_limit_bytes=VMEM_BYTES),
    )(place, block)


def pair_piece(keep, got, j):
    return jnp.concatenate([keep[j], got[j]], axis=0)


def partial_kernel(order, keep, got, cot_keep, cot_got, *refs):
    weights, refs = refs[: len(order)], refs[len(order) :]
    total = refs[0][...] if len(order) == 1 else None
    for j, weight in zip(order, weights):
        index = j if len(order) > 1 else 0
        both = jnp.concatenate([weight[0], weight[1]], axis=1)
        term = jnp.concatenate(
            [
                matmul(pair_piece(keep, got, index), both),
                matmul(pair_piece(cot_keep, cot_got, index), weight[2]),
            ],
            axis=1,
        )
        total = term if total is None else total + term
    if len(order) == 1:
        refs[1][...] = total
        refs[2][...] = total.astype(jnp.bfloat16)
    else:
        refs[0][...] = total


def partial_sums(pieces, weights, order, base=()):
    layers, rows, width = pieces[0].shape
    columns = 3 * weights[0].shape[2]
    weight = pl.BlockSpec((3, *weights[0].shape[1:]), lambda i: (0, 0, 0))
    if base:
        piece = pl.BlockSpec((1, rows, width), lambda i: (order[0], 0, 0))
    else:
        piece = pl.BlockSpec(pieces[0].shape, lambda i: (0, 0, 0))
    sums = pl.BlockSpec((2 * rows, columns), lambda i: (0, 0))
    exact = jax.ShapeDtypeStruct((2 * rows, columns), jnp.float32)
    narrow = jax.ShapeDtypeStruct((2 * rows, columns), jnp.bfloat16)
    return pl.pallas_call(
        functools.partial(partial_kernel, order),
        grid=(1,),
        in_specs=[piece] * 4 + [weight] * len(order) + [sums] * len(base),
        out_specs=[sums, sums] if base else [sums],
        out_shape=[exact, narrow] if base else [exact],
        cost_estimate=pl.CostEstimate(
            flops=4 * len(order) * rows * width * columns,
            bytes_accessed=2 * len(order) * width * (4 * rows + columns),
            transcendentals=0,
        ),
        compiler_params=pltpu.CompilerParams(vmem_limit_bytes=VMEM_BYTES),
    )(*pieces, *[weights[j] for j in order], *base)


def terms_kernel(partial, passed, keep, got, cot_keep, cot_got, own, *terms):
    rows = partial.shape[0] // 2
    half_f = partial.shape[1] // 3
    swapped = jnp.concatenate([passed[rows:], passed[:rows]], axis=0).astype(jnp.float32)
    sums = partial[...] + swapped
    hidden, gate_grad, up_grad = swiglu_back(
        sums[:, :half_f], sums[:, half_f : 2 * half_f], sums[:, 2 * half_f :]
    )
    grads = jnp.concatenate(
        [gate_grad.astype(jnp.float32).T, up_grad.astype(jnp.float32).T], axis=0
    ).astype(jnp.bfloat16)
    hidden = hidden.astype(jnp.float32).T.astype(jnp.bfloat16)
    for j, out in enumerate((own,) + terms):
        normed = pair_piece(keep, got, j)
        cotangent = pair_piece(cot_keep, cot_got, j)
        term = jnp.concatenate([matmul(grads, normed), matmul(hidden, cotangent)], axis=0)
        out[...] = term.astype(out.dtype)


def gradient_terms(partial, passed, pieces):
    layers, rows, width = pieces[0].shape
    columns = partial.shape[1]
    own = jax.ShapeDtypeStruct((columns, width), jnp.float32)
    term = jax.ShapeDtypeStruct((columns, width), jnp.bfloat16)
    return pl.pallas_call(
        terms_kernel,
        in_specs=whole(6),
        out_specs=whole(layers),
        out_shape=[own] + [term] * (layers - 1),
        cost_estimate=pl.CostEstimate(
            flops=4 * layers * rows * width * columns,
            bytes_accessed=layers * width * (8 * rows + 2 * columns),
            transcendentals=2 * rows * columns,
        ),
        compiler_params=pltpu.CompilerParams(vmem_limit_bytes=VMEM_BYTES),
    )(partial, passed, *pieces)


class Ring:
    def __init__(self, up, down):
        self.ends = [up, down]

    def go(self):
        self.ends = [shifted(self.ends[0], "z", 1), shifted(self.ends[1], "z", -1)]
        return self.ends

    def tied(self, *arrays):
        together = tie(*self.ends, *arrays)
        self.ends = list(together[:2])
        return together[2:]


def scatter_ring(terms, far, after):
    layers = len(terms)
    half = layers // 2
    routes = {1: list(range(half, 0, -1)), -1: list(range(half, layers))}
    routes[-far] = routes[-far][1:]
    sums = {1: None, -1: None}
    for step in range(half):
        for way in (1, -1):
            if step < len(routes[way]):
                term = terms[routes[way][step]]
                if sums[way] is not None:
                    term = term.astype(jnp.float32) + sums[way].astype(jnp.float32)
                sums[way] = shifted(term.astype(jnp.bfloat16), "z", way)
        sums[1], sums[-1] = after(step, sums[1], sums[-1])
    return sums[1], sums[-1]


def close_kernel(carried, *refs):
    sums, out = refs[:-1], refs[-1]
    count = carried.shape[0]
    for which in range(len(sums) // 3):
        own, up, down = sums[3 * which : 3 * which + 3]
        total = own[...] + up[...].astype(jnp.float32) + down[...].astype(jnp.float32)
        half_f = total.shape[0] // count
        columns = slice(which * half_f, (which + 1) * half_f)
        for i in range(count):
            turned = total[i * half_f : (i + 1) * half_f].T
            out[i, :, columns] = carried[i, :, columns].astype(jnp.float32) + turned


def close(carried, sums):
    size = carried.size
    return pl.pallas_call(
        close_kernel,
        in_specs=whole(1 + len(sums)),
        out_specs=pl.BlockSpec(memory_space=pltpu.VMEM),
        out_shape=jax.ShapeDtypeStruct(carried.shape, jnp.float32),
        cost_estimate=pl.CostEstimate(flops=3 * size, bytes_accessed=14 * size, transcendentals=0),
        compiler_params=pltpu.CompilerParams(vmem_limit_bytes=VMEM_BYTES),
    )(carried, *sums)


def attend_kernel(layers, place, own, other, *refs):
    pieces, (mine, theirs) = refs[:layers], refs[layers:]
    rows = own.shape[0]
    layer, side = place[0], place[1]
    length = 2 * rows
    exponent_scale = HD ** (-0.5) * math.log2(math.e)
    row = lax.broadcasted_iota(jnp.int32, (2 * rows, length), 0)
    column = lax.broadcasted_iota(jnp.int32, (2 * rows, length), 1)
    position = jnp.where(row < rows, row + side * rows, row - side * rows)
    diagonal = jnp.where(column <= position, 0.0, NEGATIVE)
    biases = [jnp.where(layer + j >= layers, 0.0, NEGATIVE) for j in range(1, layers)]

    def head(h, carry):
        columns = pl.ds(pl.multiple_of(h * HD, HD), HD)
        query = jnp.concatenate([own[:, columns], other[:, columns]], axis=0)
        scores = []
        for j, piece in enumerate(pieces):
            score = lax.dot_general(
                query, piece[0, :length], (((1,), (1,)), ((), ())), preferred_element_type=jnp.float32
            )
            scores.append(score + (diagonal if j == 0 else biases[j - 1]))
        largest = functools.reduce(jnp.maximum, scores)
        largest = jnp.max(largest, axis=1, keepdims=True)
        total = jnp.zeros((2 * rows, length), jnp.float32)
        result = jnp.zeros((2 * rows, HD), jnp.float32)
        for score, piece in zip(scores, pieces):
            probs = jnp.exp2((score - largest) * exponent_scale)
            total = total + probs
            result = result + jnp.dot(
                probs.astype(jnp.bfloat16), piece[0, length:], preferred_element_type=jnp.float32
            )
        result = (result / jnp.sum(total, axis=1, keepdims=True)).astype(jnp.bfloat16)
        mine[:, columns] = result[:rows]
        theirs[:, columns] = result[rows:]
        return carry

    lax.fori_loop(0, own.shape[1] // HD, head, 0, unroll=4)


def attend(own, other, pieces, place, part, parts):
    rows, columns = own.shape
    layers = len(pieces)
    share = columns // parts
    block = pl.BlockSpec((rows, share), lambda i: (0, part))
    out_block = pl.BlockSpec((rows, share), lambda i: (0, 0))
    kv_blocks = [
        pl.BlockSpec(
            (1, *piece.shape[1:]),
            lambda i, last=piece.shape[0] - 1: (last, 0, 0),
        )
        for piece in pieces
    ]
    length = 2 * rows
    return pl.pallas_call(
        functools.partial(attend_kernel, layers),
        grid=(1,),
        in_specs=[pl.BlockSpec(memory_space=pltpu.SMEM), block, block] + kv_blocks,
        out_specs=[out_block, out_block],
        out_shape=[jax.ShapeDtypeStruct((rows, share), jnp.bfloat16)] * 2,
        cost_estimate=pl.CostEstimate(
            flops=8 * rows * share * layers * length,
            bytes_accessed=8 * rows * share + 4 * layers * length * HD,
            transcendentals=2 * rows * share // HD * layers * length,
        ),
        compiler_params=pltpu.CompilerParams(vmem_limit_bytes=VMEM_BYTES),
    )(place, own, other, *pieces)


def shards(saved_input, output_grad, weight_span, grad_carry, attn_queries, attn_keys, attn_values):
    side = lax.axis_index("x")
    layer = lax.axis_index("z")
    layers = lax.axis_size("z")
    place = jnp.stack([layer, side]).astype(jnp.int32)

    hop0, hop1 = cut(jnp.transpose(weight_span[0], (1, 0, 2)))
    hop0, hop1, attn_keys, attn_values = tie(hop0, hop1, attn_keys, attn_values)
    arrived = [shifted(hop0, "blk", 1), shifted(hop1, "blk", 1)]

    def stacked(low):
        return [
            jnp.stack([array[0, :, k * HD : (k + 1) * HD] for array in (attn_keys, attn_values)])
            for k in range(low, low + KVH // 2)
        ]

    lower, upper = jnp.stack(stacked(0)), jnp.stack(stacked(KVH // 2))
    low = side == 0
    pair_keep, pair_give = jnp.where(low, lower, upper), jnp.where(low, upper, lower)
    pair_got = shifted(pair_give, "x", 1)

    tokens = jnp.concatenate(
        [jnp.where(low, pair_keep, pair_got), jnp.where(low, pair_got, pair_keep)], axis=2
    )
    tokens = tokens.reshape(KVH // 2, -1, HD)
    query_keep, query_give = pair_split(attn_queries[0], side)
    saved_input, output_grad, tokens = tie(saved_input, output_grad, tokens)
    arrived[1], query_give = tie(arrived[1], query_give)
    query_got = shifted(query_give, "x", 1)
    normed_keep, normed_give = feature_split(saved_input[0], place, layers, True)
    grad_keep, grad_give = feature_split(output_grad[0], place, layers, False)

    shares = []

    def share(*arrays):
        *arrays, queries = tie(*arrays, query_keep)
        head = heads[len(shares) // 2]
        pieces = [head[j] for j in range(layers)]
        mine, theirs = attend(queries, query_got, pieces, place, len(shares), 4)
        shares.append([mine, theirs])
        return arrays

    def kept(ring, found, step):
        found[layers - step], found[step] = ring.go()

    steps = layers // 2
    heads = [{0: tokens[k : k + 1]} for k in range(2)]
    arrived[0], tokens, normed_give, grad_give = tie(arrived[0], tokens, normed_give, grad_give)
    halves = [{0: part} for part in arrived]
    blocks = [jnp.concatenate([arrived[k], tokens[k : k + 1]]) for k in range(2)]
    rings = [Ring(block, block) for block in blocks]
    for step in range(1, steps):
        for k in range(2):
            kept(rings[k], halves[k], step)
            heads[k][layers - step], heads[k][step] = halves[k][layers - step], halves[k][step]
            if k == 0 and step == 1:
                query_got, normed_give = rings[0].tied(query_got, normed_give)
                normed_got = shifted(normed_give, "x", 1)
            elif k == 0 and step == 2:
                (grad_give,) = rings[0].tied(grad_give)
                grad_got = shifted(grad_give, "x", 1)
            elif k == 1 and step == 2:
                (normed_got,) = rings[1].tied(normed_got)
            elif k == 1 and step == 3:
                (grad_got,) = rings[1].tied(grad_got)
    halves[0][steps] = heads[0][steps] = shifted(rings[0].ends[0], "z", 1)
    halves[1][steps] = heads[1][steps] = shifted(rings[1].ends[1], "z", -1)

    pieces = (normed_keep, normed_got, grad_keep, grad_got)
    exacts, passed = [], []
    for found in halves:
        base = partial_sums(pieces, found, [j for j in range(layers) if j != steps])
        exact, narrow = partial_sums(pieces, found, [steps], tuple(base))
        exacts.append(exact)
        (narrow,) = share(narrow)
        got, shares[-1][0] = tie(shifted(narrow, "x", 1), shares[-1][0])
        passed.append(got)
    passed[1], grad_carry = tie(passed[1], grad_carry)
    carried = [shifted(jnp.transpose(grad_carry[0], (1, 0, 2)).astype(jnp.bfloat16), "blk", -1)]

    def plain(step, *arrays):
        return arrays

    def after(step, *arrays):
        if step == 1:
            *arrays, carried[0] = tie(*arrays, carried[0])
        if step in (1, 2):
            *arrays, shares[-1][0] = tie(*arrays, shares[-1][0])
        if step in (0, 1):
            arrays = share(*arrays)
        return arrays

    outs = []
    for which in range(2):
        own, *terms = gradient_terms(exacts[which], passed[which], pieces)
        outs += [own, *scatter_ring([None] + terms, 1 - 2 * which, after if which == 1 else plain)]
    carry_out = jnp.transpose(close(carried[0], outs), (1, 0, 2))[None]

    mine = jnp.concatenate([piece[0] for piece in shares], axis=1)
    got = shifted(jnp.concatenate([piece[1] for piece in shares], axis=1), "x", 1)
    attn_out = jnp.concatenate([jnp.where(low, mine, got), jnp.where(low, got, mine)], axis=1)
    return (carry_out, attn_out[None])


def solution(mesh):
    workers, parts = mesh.devices.shape
    split = Mesh(mesh.devices.reshape(workers, parts // 2, 2), ("blk", "z", "x"))
    seq = ("z", "x")
    return jax.shard_map(
        shards,
        mesh=split,
        in_specs=(
            P("blk", seq, None),
            P("blk", seq, None),
            P("blk", seq, None, None),
            P("blk", seq, None, None),
            P("blk", seq, None),
            P("blk", seq, None),
            P("blk", seq, None),
        ),
        out_specs=(P("blk", seq, None, None), P("blk", seq, None)),
        check_vma=False,
    )
```

```python
import functools
import math

import jax
import jax.numpy as jnp
from jax import lax
from jax.experimental import pallas as pl
from jax.experimental.pallas import tpu as pltpu
from jax.sharding import Mesh, PartitionSpec as P

HD = 128
QH = 32
KVH = 4

EPSILON = 1e-05
NEGATIVE = -1e30


def shifted(block, axis, distance):
    devices = range(lax.axis_size(axis))
    route = [((i - distance) % len(devices), i) for i in devices]
    return lax.ppermute(block, axis, route)


def matmul(left, right):
    return jnp.dot(left, right, preferred_element_type=jnp.float32)


def swiglu_back(gate_sum, up_sum, hidden_grad):
    sigmoid_gate = jax.nn.sigmoid(gate_sum)
    activated = gate_sum * sigmoid_gate
    hidden = (activated * up_sum).astype(jnp.bfloat16)
    up_grad = (hidden_grad * activated).astype(jnp.bfloat16)
    gate_grad = (
        hidden_grad * up_sum * sigmoid_gate * (1.0 + gate_sum * (1.0 - sigmoid_gate))
    ).astype(jnp.bfloat16)
    return (hidden, gate_grad, up_grad)


def pair_split(block, side):
    rows, columns = block.shape
    low, high = block[:, : columns // 2], block[:, columns // 2 :]
    first = side == 0
    return jnp.where(first, low, high), jnp.where(first, high, low)


def pair_rows(own, other, side):
    first = side == 0
    return jnp.concatenate([jnp.where(first, own, other), jnp.where(first, other, own)], axis=0)


def tie(*arrays):
    return lax.optimization_barrier(arrays)


VMEM_BYTES = 40 * 1024 * 1024


def whole(count):
    return [pl.BlockSpec(memory_space=pltpu.VMEM)] * count


def cut_kernel(span, low, high, arrivals):
    half = low.shape[2]
    copies = [
        pltpu.make_async_copy(span.at[:, :, k * half : (k + 1) * half], out, arrivals.at[k])
        for k, out in enumerate((low, high))
    ]
    for copy in copies:
        copy.start()
    for copy in copies:
        copy.wait()


def cut(span):
    half = jax.ShapeDtypeStruct((*span.shape[:2], span.shape[2] // 2), span.dtype)
    anywhere = pl.BlockSpec(memory_space=pl.ANY)
    return pl.pallas_call(
        cut_kernel,
        in_specs=[anywhere],
        out_specs=[anywhere, anywhere],
        out_shape=[half, half],
        scratch_shapes=[pltpu.SemaphoreType.DMA((2,))],
        cost_estimate=pl.CostEstimate(flops=0, bytes_accessed=4 * span.size, transcendentals=0),
        compiler_params=pltpu.CompilerParams(vmem_limit_bytes=VMEM_BYTES),
    )(span)


def split_kernel(layers, normalized, place, block, keep, give):
    layer, side = place[0], place[1]
    rows, columns = block.shape
    width = columns // layers // 2
    if normalized:
        total = jnp.zeros((rows, width), jnp.float32)
        for k in range(2 * layers):
            widened = block[:, k * width : (k + 1) * width].astype(jnp.float32)
            total = total + widened * widened
        factor = lax.rsqrt(jnp.sum(total, axis=1, keepdims=True) / columns + EPSILON)
    for j in range(layers):
        first = ((layer + j) % layers) * (2 * width)
        for out, which in ((keep, side), (give, 1 - side)):
            start = pl.multiple_of(first + which * width, width)
            piece = block[:, pl.ds(start, width)]
            if normalized:
                piece = (piece.astype(jnp.float32) * factor).astype(jnp.bfloat16)
            out[j] = piece


def feature_split(block, place, layers, normalized):
    rows, columns = block.shape
    shape = jax.ShapeDtypeStruct((layers, rows, columns // layers // 2), jnp.bfloat16)
    return pl.pallas_call(
        functools.partial(split_kernel, layers, normalized),
        in_specs=[pl.BlockSpec(memory_space=pltpu.SMEM)] + whole(1),
        out_specs=whole(2),
        out_shape=[shape, shape],
        cost_estimate=pl.CostEstimate(
            flops=4 * rows * columns, bytes_accessed=4 * rows * columns, transcendentals=0
        ),
        compiler_params=pltpu.CompilerParams(vmem_limit_bytes=VMEM_BYTES),
    )(place, block)


def pair_piece(keep, got, j):
    return jnp.concatenate([keep[j], got[j]], axis=0)


def partial_kernel(order, keep, got, cot_keep, cot_got, *refs):
    weights, refs = refs[: len(order)], refs[len(order) :]
    total = refs[0][...] if len(order) == 1 else None
    for j, weight in zip(order, weights):
        index = j if len(order) > 1 else 0
        both = jnp.concatenate([weight[0], weight[1]], axis=1)
        term = jnp.concatenate(
            [
                matmul(pair_piece(keep, got, index), both),
                matmul(pair_piece(cot_keep, cot_got, index), weight[2]),
            ],
            axis=1,
        )
        total = term if total is None else total + term
    if len(order) == 1:
        refs[1][...] = total
        refs[2][...] = total.astype(jnp.bfloat16)
    else:
        refs[0][...] = total


def partial_sums(pieces, weights, order, base=()):
    layers, rows, width = pieces[0].shape
    columns = 3 * weights[0].shape[2]
    weight = pl.BlockSpec((3, *weights[0].shape[1:]), lambda i: (0, 0, 0))
    if base:
        piece = pl.BlockSpec((1, rows, width), lambda i: (order[0], 0, 0))
    else:
        piece = pl.BlockSpec(pieces[0].shape, lambda i: (0, 0, 0))
    sums = pl.BlockSpec((2 * rows, columns), lambda i: (0, 0))
    exact = jax.ShapeDtypeStruct((2 * rows, columns), jnp.float32)
    narrow = jax.ShapeDtypeStruct((2 * rows, columns), jnp.bfloat16)
    return pl.pallas_call(
        functools.partial(partial_kernel, order),
        grid=(1,),
        in_specs=[piece] * 4 + [weight] * len(order) + [sums] * len(base),
        out_specs=[sums, sums] if base else [sums],
        out_shape=[exact, narrow] if base else [exact],
        cost_estimate=pl.CostEstimate(
            flops=4 * len(order) * rows * width * columns,
            bytes_accessed=2 * len(order) * width * (4 * rows + columns),
            transcendentals=0,
        ),
        compiler_params=pltpu.CompilerParams(vmem_limit_bytes=VMEM_BYTES),
    )(*pieces, *[weights[j] for j in order], *base)


def pair_term(grads, hidden, keep, got, cot_keep, cot_got, j):
    return jnp.concatenate(
        [
            matmul(grads, pair_piece(keep, got, j)),
            matmul(hidden, pair_piece(cot_keep, cot_got, j)),
        ],
        axis=0,
    )


def first_terms_kernel(order, partial, passed, keep, got, cot_keep, cot_got, grads, hidden, *terms):
    rows = partial.shape[0] // 2
    half_f = partial.shape[1] // 3
    swapped = jnp.concatenate([passed[rows:], passed[:rows]], axis=0).astype(jnp.float32)
    sums = partial[...] + swapped
    inner, gate_grad, up_grad = swiglu_back(
        sums[:, :half_f], sums[:, half_f : 2 * half_f], sums[:, 2 * half_f :]
    )
    turned = jnp.concatenate(
        [gate_grad.astype(jnp.float32).T, up_grad.astype(jnp.float32).T], axis=0
    ).astype(jnp.bfloat16)
    inner = inner.astype(jnp.float32).T.astype(jnp.bfloat16)
    grads[...] = turned
    hidden[...] = inner
    for j, out in zip(order, terms):
        out[...] = pair_term(turned, inner, keep, got, cot_keep, cot_got, j).astype(out.dtype)


def other_terms_kernel(order, grads, hidden, keep, got, cot_keep, cot_got, *terms):
    for j, out in zip(order, terms):
        term = pair_term(grads[...], hidden[...], keep, got, cot_keep, cot_got, j)
        out[...] = term.astype(out.dtype)


def gradient_terms(partial, passed, pieces, first):
    layers, rows, width = pieces[0].shape
    columns = partial.shape[1]
    own = jax.ShapeDtypeStruct((columns, width), jnp.float32)
    term = jax.ShapeDtypeStruct((columns, width), jnp.bfloat16)
    others = [j for j in range(layers) if j not in first]
    turned = [
        jax.ShapeDtypeStruct((columns * part // 3, 2 * rows), jnp.bfloat16) for part in (2, 1)
    ]
    params = pltpu.CompilerParams(vmem_limit_bytes=VMEM_BYTES)

    def cost(count):
        return pl.CostEstimate(
            flops=4 * count * rows * width * columns,
            bytes_accessed=count * width * (8 * rows + 2 * columns),
            transcendentals=2 * rows * columns,
        )

    grads, hidden, *early = pl.pallas_call(
        functools.partial(first_terms_kernel, first),
        in_specs=whole(6),
        out_specs=whole(2 + len(first)),
        out_shape=turned + [term] * len(first),
        cost_estimate=cost(len(first)),
        compiler_params=params,
    )(partial, passed, *pieces)
    late = pl.pallas_call(
        functools.partial(other_terms_kernel, others),
        in_specs=whole(6),
        out_specs=whole(len(others)),
        out_shape=[own if j == 0 else term for j in others],
        cost_estimate=cost(len(others)),
        compiler_params=params,
    )(grads, hidden, *pieces)
    found = dict(zip(list(first) + others, list(early) + list(late)))
    return [found[j] for j in range(layers)]


class Ring:
    def __init__(self, up, down):
        self.ends = [up, down]

    def go(self):
        self.ends = [shifted(self.ends[0], "z", 1), shifted(self.ends[1], "z", -1)]
        return self.ends

    def tied(self, *arrays):
        together = tie(*self.ends, *arrays)
        self.ends = list(together[:2])
        return together[2:]


def scatter_ring(terms, far, after):
    layers = len(terms)
    half = layers // 2
    routes = {1: list(range(half, 0, -1)), -1: list(range(half, layers))}
    routes[-far] = routes[-far][1:]
    sums = {1: None, -1: None}
    for step in range(half):
        for way in (1, -1):
            if step < len(routes[way]):
                term = terms[routes[way][step]]
                if sums[way] is not None:
                    term = term.astype(jnp.float32) + sums[way].astype(jnp.float32)
                sums[way] = shifted(term.astype(jnp.bfloat16), "z", way)
        sums[1], sums[-1] = after(step, sums[1], sums[-1])
    return sums[1], sums[-1]


def close_kernel(carried, *refs):
    sums, out = refs[:-1], refs[-1]
    count = carried.shape[0]
    for which in range(len(sums) // 3):
        own, up, down = sums[3 * which : 3 * which + 3]
        total = own[...] + up[...].astype(jnp.float32) + down[...].astype(jnp.float32)
        half_f = total.shape[0] // count
        columns = slice(which * half_f, (which + 1) * half_f)
        for i in range(count):
            turned = total[i * half_f : (i + 1) * half_f].T
            out[i, :, columns] = carried[i, :, columns].astype(jnp.float32) + turned


def close(carried, sums):
    size = carried.size
    return pl.pallas_call(
        close_kernel,
        in_specs=whole(1 + len(sums)),
        out_specs=pl.BlockSpec(memory_space=pltpu.VMEM),
        out_shape=jax.ShapeDtypeStruct(carried.shape, jnp.float32),
        cost_estimate=pl.CostEstimate(flops=3 * size, bytes_accessed=14 * size, transcendentals=0),
        compiler_params=pltpu.CompilerParams(vmem_limit_bytes=VMEM_BYTES),
    )(carried, *sums)


def attend_kernel(layers, place, own, other, *refs):
    pieces, (mine, theirs) = refs[:layers], refs[layers:]
    rows = own.shape[0]
    layer, side = place[0], place[1]
    length = 2 * rows
    exponent_scale = HD ** (-0.5) * math.log2(math.e)
    row = lax.broadcasted_iota(jnp.int32, (2 * rows, length), 0)
    column = lax.broadcasted_iota(jnp.int32, (2 * rows, length), 1)
    position = jnp.where(row < rows, row + side * rows, row - side * rows)
    diagonal = jnp.where(column <= position, 0.0, NEGATIVE)
    biases = [jnp.where(layer + j >= layers, 0.0, NEGATIVE) for j in range(1, layers)]

    def head(h, carry):
        columns = pl.ds(pl.multiple_of(h * HD, HD), HD)
        query = jnp.concatenate([own[:, columns], other[:, columns]], axis=0)
        scores = []
        for j, piece in enumerate(pieces):
            score = lax.dot_general(
                query, piece[0, :length], (((1,), (1,)), ((), ())), preferred_element_type=jnp.float32
            )
            scores.append(score + (diagonal if j == 0 else biases[j - 1]))
        largest = functools.reduce(jnp.maximum, scores)
        largest = jnp.max(largest, axis=1, keepdims=True)
        total = jnp.zeros((2 * rows, length), jnp.float32)
        result = jnp.zeros((2 * rows, HD), jnp.float32)
        for score, piece in zip(scores, pieces):
            probs = jnp.exp2((score - largest) * exponent_scale)
            total = total + probs
            result = result + jnp.dot(
                probs.astype(jnp.bfloat16), piece[0, length:], preferred_element_type=jnp.float32
            )
        result = (result / jnp.sum(total, axis=1, keepdims=True)).astype(jnp.bfloat16)
        mine[:, columns] = result[:rows]
        theirs[:, columns] = result[rows:]
        return carry

    lax.fori_loop(0, own.shape[1] // HD, head, 0, unroll=4)


def attend(own, other, pieces, place, part, parts):
    rows, columns = own.shape
    layers = len(pieces)
    share = columns // parts
    block = pl.BlockSpec((rows, share), lambda i: (0, part))
    out_block = pl.BlockSpec((rows, share), lambda i: (0, 0))
    kv_blocks = [
        pl.BlockSpec(
            (1, *piece.shape[1:]),
            lambda i, last=piece.shape[0] - 1: (last, 0, 0),
        )
        for piece in pieces
    ]
    length = 2 * rows
    return pl.pallas_call(
        functools.partial(attend_kernel, layers),
        grid=(1,),
        in_specs=[pl.BlockSpec(memory_space=pltpu.SMEM), block, block] + kv_blocks,
        out_specs=[out_block, out_block],
        out_shape=[jax.ShapeDtypeStruct((rows, share), jnp.bfloat16)] * 2,
        cost_estimate=pl.CostEstimate(
            flops=8 * rows * share * layers * length,
            bytes_accessed=8 * rows * share + 4 * layers * length * HD,
            transcendentals=2 * rows * share // HD * layers * length,
        ),
        compiler_params=pltpu.CompilerParams(vmem_limit_bytes=VMEM_BYTES),
    )(place, own, other, *pieces)


def shards(saved_input, output_grad, weight_span, grad_carry, attn_queries, attn_keys, attn_values):
    side = lax.axis_index("x")
    layer = lax.axis_index("z")
    layers = lax.axis_size("z")
    place = jnp.stack([layer, side]).astype(jnp.int32)

    hop0, hop1 = cut(jnp.transpose(weight_span[0], (1, 0, 2)))
    hop0, hop1, attn_keys, attn_values = tie(hop0, hop1, attn_keys, attn_values)
    arrived = [shifted(hop0, "blk", 1), shifted(hop1, "blk", 1)]

    def stacked(low):
        return [
            jnp.stack([array[0, :, k * HD : (k + 1) * HD] for array in (attn_keys, attn_values)])
            for k in range(low, low + KVH // 2)
        ]

    lower, upper = jnp.stack(stacked(0)), jnp.stack(stacked(KVH // 2))
    low = side == 0
    pair_keep, pair_give = jnp.where(low, lower, upper), jnp.where(low, upper, lower)
    pair_got = shifted(pair_give, "x", 1)

    tokens = jnp.concatenate(
        [jnp.where(low, pair_keep, pair_got), jnp.where(low, pair_got, pair_keep)], axis=2
    )
    tokens = tokens.reshape(KVH // 2, -1, HD)
    query_keep, query_give = pair_split(attn_queries[0], side)
    saved_input, output_grad, tokens = tie(saved_input, output_grad, tokens)
    arrived[1], query_give = tie(arrived[1], query_give)
    query_got = shifted(query_give, "x", 1)
    normed_keep, normed_give = feature_split(saved_input[0], place, layers, True)
    grad_keep, grad_give = feature_split(output_grad[0], place, layers, False)

    shares = []

    def share(*arrays):
        *arrays, queries = tie(*arrays, query_keep)
        head = heads[len(shares) // 2]
        pieces = [head[j] for j in range(layers)]
        mine, theirs = attend(queries, query_got, pieces, place, len(shares), 4)
        shares.append([mine, theirs])
        return arrays

    def kept(ring, found, step):
        found[layers - step], found[step] = ring.go()

    steps = layers // 2
    heads = [{0: tokens[k : k + 1]} for k in range(2)]
    arrived[0], tokens, normed_give, grad_give = tie(arrived[0], tokens, normed_give, grad_give)
    halves = [{0: part} for part in arrived]
    blocks = [jnp.concatenate([arrived[k], tokens[k : k + 1]]) for k in range(2)]
    rings = [Ring(block, block) for block in blocks]
    for step in range(1, steps):
        for k in range(2):
            kept(rings[k], halves[k], step)
            heads[k][layers - step], heads[k][step] = halves[k][layers - step], halves[k][step]
            if k == 0 and step == 1:
                query_got, normed_give = rings[0].tied(query_got, normed_give)
                normed_got = shifted(normed_give, "x", 1)
            elif k == 0 and step == 2:
                (grad_give,) = rings[0].tied(grad_give)
                grad_got = shifted(grad_give, "x", 1)
            elif k == 1 and step == 2:
                (normed_got,) = rings[1].tied(normed_got)
            elif k == 1 and step == 3:
                (grad_got,) = rings[1].tied(grad_got)
    halves[0][steps] = heads[0][steps] = shifted(rings[0].ends[0], "z", 1)
    halves[1][steps] = heads[1][steps] = shifted(rings[1].ends[1], "z", -1)

    pieces = (normed_keep, normed_got, grad_keep, grad_got)
    exacts, passed = [], []
    for found in halves:
        base = partial_sums(pieces, found, [j for j in range(layers) if j != steps])
        exact, narrow = partial_sums(pieces, found, [steps], tuple(base))
        exacts.append(exact)
        (narrow,) = share(narrow)
        got, shares[-1][0] = tie(shifted(narrow, "x", 1), shares[-1][0])
        passed.append(got)
    passed[1], grad_carry = tie(passed[1], grad_carry)
    carried = [shifted(jnp.transpose(grad_carry[0], (1, 0, 2)).astype(jnp.bfloat16), "blk", -1)]

    def plain(step, *arrays):
        return arrays

    def after(step, *arrays):
        if step == 1:
            *arrays, carried[0] = tie(*arrays, carried[0])
        if step in (1, 2):
            *arrays, shares[-1][0] = tie(*arrays, shares[-1][0])
        if step in (0, 1):
            arrays = share(*arrays)
        return arrays

    outs = []
    for which in range(2):
        own, *terms = gradient_terms(
            exacts[which], passed[which], pieces, [steps - which, steps - which + 1]
        )
        outs += [own, *scatter_ring([None] + terms, 1 - 2 * which, after if which == 1 else plain)]
    carry_out = jnp.transpose(close(carried[0], outs), (1, 0, 2))[None]

    mine = jnp.concatenate([piece[0] for piece in shares], axis=1)
    got = shifted(jnp.concatenate([piece[1] for piece in shares], axis=1), "x", 1)
    attn_out = jnp.concatenate([jnp.where(low, mine, got), jnp.where(low, got, mine)], axis=1)
    return (carry_out, attn_out[None])


def solution(mesh):
    workers, parts = mesh.devices.shape
    split = Mesh(mesh.devices.reshape(workers, parts // 2, 2), ("blk", "z", "x"))
    seq = ("z", "x")
    return jax.shard_map(
        shards,
        mesh=split,
        in_specs=(
            P("blk", seq, None),
            P("blk", seq, None),
            P("blk", seq, None, None),
            P("blk", seq, None, None),
            P("blk", seq, None),
            P("blk", seq, None),
            P("blk", seq, None),
        ),
        out_specs=(P("blk", seq, None, None), P("blk", seq, None)),
        check_vma=False,
    )
```
